32 devices in a mesh: shot: 4 (over x, core), slab: 8 (over z, y).
Axes of the slice: x: 2, y: 2, z: 4, core: 2. Of those that a mesh axis runs over, the one named last changes fastest.
Arguments:
- lame_lambda: float32 [16, 32, 128], P('slab'), may hold values from 0.5 to 1.5
- lame_mu: float32 [16, 32, 128], P('slab'), may hold values from 0.3 to 0.8
- buoyancy: float32 [16, 32, 128], P('slab'), may hold values from 0.5 to 1
- forward_state: float32 [4, 9, 16, 32, 128], P('shot', None, 'slab'), may hold values from -6 to 6
- adjoint_state: float32 [4, 9, 16, 32, 128], P('shot', None, 'slab'), may hold values from -6 to 6
- source_wavelet: float32 [4, 8], P('shot'), may hold values from -20 to 20
- source_cell: int32 [4], P('shot'), may hold values from 0 to 65535
- residual_traces: float32 [4, 8, 1024], P('shot', None, 'slab'), may hold values from -12 to 12
- receiver_slab: int32 [1024, 1], P('slab'), may hold values from 0 to 7; in each aligned block of 128 rows (0 to 127, 128 to 255, ...) at most 32 rows name the same one
- receiver_cell: int32 [1024], P('slab'), may hold values from 0 to 8191
Outputs:
- adjoint_start: float32 [4, 9, 16, 32, 128], P('shot', None, 'slab')
- lambda_gradient: float32 [16, 32, 128], P('slab', 'shot')
- mu_gradient: float32 [16, 32, 128], P('slab', 'shot')
The draws below stay inside these ranges and needn't reach their ends.
Inputs may be any that keep to these rules, and one draw needn't show every extreme that they name: `receiver_slab`: among the 128 receivers held by one index of slab, at most 32 lie in any one slab.
All inputs are finite; a program needn't handle non-finite values.
Results may differ from the reference program's by a relative error of at most 0.000067.
Values sent between devices are 32-bit elements; how exact they have to be, the bound alone decides.
A program may use at most 64 MiB of HBM per device.

```python
import math
import jax
import jax.numpy as jnp
import numpy as np
from jax import lax

SX = 2
NY = 32
NZ = 128
REC_DEV = 128
STEPS = 8
SHOTS = 4
NX = 16
NREC = 1024
RCAP = 32
N_SLAB = 8


def plant(array, stream_key, smallest, high):
    index_at = [jax.random.randint(jax.random.fold_in(stream_key, axis), (), 0, length) for axis, length in enumerate(array.shape)]
    longest = array.shape.index(max(array.shape))
    neighbour = index_at[:longest] + [(index_at[longest] + 1) % array.shape[longest]] + index_at[longest + 1:]
    return array.at[tuple(index_at)].set(smallest).at[tuple(neighbour)].set(high)


def block_scale(rng, shape, shards, least, largest):
    def one(dim, parts):
        heights = jax.random.uniform(jax.random.fold_in(jax.random.fold_in(rng, 6), dim), (parts,), jnp.float32, least / len(shards), largest / len(shards))
        return jnp.repeat(jnp.exp(heights), shape[dim] // parts).reshape((-1,) + (1,) * (len(shape) - dim - 1))

    loudness = one(*shards[0])
    for cut in shards[1:]:
        loudness = loudness * one(*cut)
    return loudness


def assign_block(own_key, own, number, rows, number_of, top, bound, slope):
    order = jax.random.permutation(own_key, number_of)
    crowded, ordinary = load_shares(number_of, rows * top, bound, slope, True), load_shares(number_of, rows * top, bound, slope, False)
    places = jnp.arange(number_of)

    def named(lengths, rotation):
        used = int((lengths > 0).sum())
        fixed = max(1, used // 4)
        shifted = fixed + (places - fixed + rotation * (used - fixed)) % max(1, number_of - fixed)
        return jnp.zeros((number_of,), jnp.int32).at[order[jnp.where(places < fixed, places, shifted)]].set(jnp.asarray(lengths, jnp.int32))

    lengths = jnp.where(number % 4 == 0, named(crowded, number // 4), named(ordinary, number - number // 4 - 1))
    mixed = jax.random.permutation(jax.random.fold_in(own, 3), number_of)
    source_of, taker = mixed[0:number_of // 2 * 2:2], mixed[1:number_of // 2 * 2:2]
    margin = jnp.minimum(lengths[source_of] - 1, bound - lengths[taker]) // 2
    margin = jnp.where((source_of == order[0]) | (taker == order[0]) | (lengths[taker] == 0), 0, jnp.maximum(margin, 0))
    shifted = jax.random.randint(jax.random.fold_in(own, 4), (number_of // 2,), 0, 1 << 20) % (margin + 1)
    lengths = lengths.at[source_of].add(-shifted).at[taker].add(shifted)
    labels = jnp.searchsorted(jnp.cumsum(lengths), jnp.arange(rows * top), side="right").astype(jnp.int32)
    table = labels.reshape(top, rows).T
    table = table[jax.random.permutation(jax.random.fold_in(own, 1), rows)]
    rotation = jax.random.randint(jax.random.fold_in(own, 2), (rows, 1), 0, top)
    return jnp.take_along_axis(table, (jnp.arange(top)[None, :] + rotation) % top, axis=1)


def load_shares(amount, total, most, slope, full):
    portions = [(1 << 20) // math.isqrt(standing ** slope) + 1 for standing in range(1, amount + 1)]
    largest = most if full else min(most, max(-(-total // amount), total * portions[0] // sum(portions)))
    least = 1 if total - largest >= amount - 1 else 0
    counts, spare = [largest] + [least] * (amount - 1), total - largest - least * (amount - 1)
    while spare > 0:
        candidates = [i for i in range(1, amount) if counts[i] < largest] or [i for i in range(1, amount) if counts[i] < most]
        pool, budget = sum([portions[i] for i in candidates]), spare
        for i in candidates:
            extra = min(most - counts[i], max(1, budget * portions[i] // pool), spare)
            counts[i] = counts[i] + extra
            spare = spare - extra
    return np.array(counts)


def noise(rng, shape, width, limit, cuts=(), kind=jnp.bfloat16):
    drawn = jax.random.normal(rng, shape, jnp.float32) * width
    if len(cuts) > 0:
        drawn = block_scale(rng, shape, cuts, -0.22, 0.18) * drawn
    return jnp.clip(drawn, min=-limit, max=limit).astype(kind)


def setup_inputs(seed: int = 0) -> dict:
    key_of = jax.random.split(jax.random.key(seed), 11)
    lame_lambda = jnp.clip(jnp.exp(math.log(1.5) - 1.0986123 * jax.random.uniform(key_of[0], (NX, NY, NZ), jnp.float32) ** block_scale(key_of[0], (NX, NY, NZ), ((0, 8),), -0.2, 0.2)), 0.5, 1.5)
    lame_mu = jnp.clip(jnp.exp(math.log(0.8) - 0.98082923 * jax.random.uniform(key_of[1], (NX, NY, NZ), jnp.float32) ** block_scale(key_of[1], (NX, NY, NZ), ((0, 8),), -0.2, 0.2)), 0.3, 0.8)
    buoyancy = jnp.clip(jnp.exp(math.log(1.0) - 0.6931472 * jax.random.uniform(key_of[2], (NX, NY, NZ), jnp.float32) ** block_scale(key_of[2], (NX, NY, NZ), ((0, 8),), -0.2, 0.2)), 0.5, 1.0)
    forward_state = noise(key_of[3], (SHOTS, 9, NX, NY, NZ), 1.0, 6.0, ((0, 4), (2, 8)), jnp.float32)
    adjoint_state = noise(key_of[4], (SHOTS, 9, NX, NY, NZ), 1.0, 6.0, ((0, 4), (2, 8)), jnp.float32)
    source_wavelet = noise(key_of[5], (SHOTS, STEPS), 5.0, 20.0, ((0, 4),), jnp.float32)
    source_cell = plant(jax.random.randint(key_of[6], (SHOTS,), 0, NX * NY * NZ), jax.random.fold_in(key_of[6], 1), 0, (NX * NY * NZ) - 1).astype(jnp.int32)
    residual_traces = noise(key_of[7], (SHOTS, STEPS, NREC), 3.0, 12.0, ((0, 4), (2, 8)), jnp.float32)
    receiver_slab_keys = jax.random.split(jax.random.fold_in(key_of[8], 1), NREC // REC_DEV)
    receiver_slab_turns = jax.random.permutation(jax.random.fold_in(key_of[8], 3), NREC // REC_DEV)
    receiver_slab = jax.vmap(lambda own, number: assign_block(jax.random.fold_in(key_of[8], 2), own, number, REC_DEV, N_SLAB, 1, RCAP, 2))(receiver_slab_keys, receiver_slab_turns).reshape((NREC, 1))
    receiver_cell = plant(jax.random.randint(key_of[9], (NREC,), 0, SX * NY * NZ), jax.random.fold_in(key_of[9], 1), 0, (SX * NY * NZ) - 1).astype(jnp.int32)
    return dict(lame_lambda=lame_lambda, lame_mu=lame_mu, buoyancy=buoyancy, forward_state=forward_state, adjoint_state=adjoint_state, source_wavelet=source_wavelet, source_cell=source_cell, residual_traces=residual_traces, receiver_slab=receiver_slab, receiver_cell=receiver_cell)


TIME_STEP = 0.3


def next_cell(values, along):
    extent = values.shape[along]
    remainder = lax.slice_in_dim(values, 1, extent, axis=along)
    border = jnp.zeros_like(lax.slice_in_dim(values, 0, 1, axis=along))
    return jnp.concatenate([remainder, border], axis=along)


def prev_cell(values, along):
    extent = values.shape[along]
    remainder = lax.slice_in_dim(values, 0, extent - 1, axis=along)
    border = jnp.zeros_like(lax.slice_in_dim(values, 0, 1, axis=along))
    return jnp.concatenate([border, remainder], axis=along)


def velocity_update(velocity, stress, buoyancy, normal_after, shear_before):
    sigma_xx = stress[:, 0]
    sigma_yy = stress[:, 1]
    sigma_zz = stress[:, 2]
    sigma_xy = stress[:, 3]
    sigma_xz = stress[:, 4]
    sigma_yz = stress[:, 5]
    accel_x = (normal_after - sigma_xx) + (sigma_xy - prev_cell(sigma_xy, 2)) + (sigma_xz - prev_cell(sigma_xz, 3))
    accel_y = (sigma_xy - shear_before[:, 0]) + (next_cell(sigma_yy, 2) - sigma_yy) + (sigma_yz - prev_cell(sigma_yz, 3))
    accel_z = (sigma_xz - shear_before[:, 1]) + (sigma_yz - prev_cell(sigma_yz, 2)) + (next_cell(sigma_zz, 3) - sigma_zz)
    factor = TIME_STEP * buoyancy
    return jnp.stack([velocity[:, 0] - factor * accel_x, velocity[:, 1] - factor * accel_y, velocity[:, 2] - factor * accel_z], axis=1)


def stress_update(velocity, stress, lame_lambda, lame_mu, speed_before, speeds_after):
    speed_x = velocity[:, 0]
    speed_y = velocity[:, 1]
    speed_z = velocity[:, 2]
    strain_xx = speed_x - speed_before[:, 0]
    strain_yy = speed_y - prev_cell(speed_y, 2)
    strain_zz = speed_z - prev_cell(speed_z, 3)
    strain_xy = (next_cell(speed_x, 2) - speed_x) + (speeds_after[:, 0] - speed_y)
    strain_xz = (next_cell(speed_x, 3) - speed_x) + (speeds_after[:, 1] - speed_z)
    strain_yz = (next_cell(speed_y, 3) - speed_y) + (next_cell(speed_z, 2) - speed_z)
    dilation = strain_xx + strain_yy + strain_zz
    volume_term = lame_lambda * dilation
    twice_mu = 2.0 * lame_mu
    updated = jnp.stack([
        stress[:, 0] - TIME_STEP * (volume_term + twice_mu * strain_xx),
        stress[:, 1] - TIME_STEP * (volume_term + twice_mu * strain_yy),
        stress[:, 2] - TIME_STEP * (volume_term + twice_mu * strain_zz),
        stress[:, 3] - TIME_STEP * (lame_mu * strain_xy),
        stress[:, 4] - TIME_STEP * (lame_mu * strain_xz),
        stress[:, 5] - TIME_STEP * (lame_mu * strain_yz)], axis=1)
    return updated, (strain_xx, strain_yy, strain_zz, strain_xy, strain_xz, strain_yz)


def imaging(strains):
    strain_xx, strain_yy, strain_zz, strain_xy, strain_xz, strain_yz = strains
    dilation = strain_xx + strain_yy + strain_zz
    lambda_term = TIME_STEP * (dilation[0] * dilation[1])
    shear_term = 2.0 * (strain_xx[0] * strain_xx[1] + strain_yy[0] * strain_yy[1] + strain_zz[0] * strain_zz[1])
    shear_term = shear_term + strain_xy[0] * strain_xy[1] + strain_xz[0] * strain_xz[1] + strain_yz[0] * strain_yz[1]
    return lambda_term, TIME_STEP * shear_term


def reference(lame_lambda, lame_mu, buoyancy, forward_state, adjoint_state, source_wavelet, source_cell, residual_traces, receiver_slab, receiver_cell):
    extent_x, extent_y, extent_z = lame_lambda.shape
    total_cells = extent_x * extent_y * extent_z
    slab_cells = SX * NY * NZ
    targets = (receiver_slab[:, 0] * slab_cells + receiver_cell).astype(jnp.int32)
    grad_lambda = jnp.zeros(lame_lambda.shape, jnp.float32)
    grad_shear = jnp.zeros(lame_lambda.shape, jnp.float32)
    finals = []
    for shot_index in range(SHOTS):
        receiver_push = jnp.zeros((STEPS, total_cells), jnp.float32).at[:, targets].add(residual_traces[shot_index])
        receiver_push = receiver_push.reshape(STEPS, extent_x, extent_y, extent_z)
        source_spot = (jnp.arange(total_cells, dtype=jnp.int32) == source_cell[shot_index]).astype(jnp.float32).reshape(extent_x, extent_y, extent_z)
        wavefields = jnp.stack([forward_state[shot_index], adjoint_state[shot_index]])
        velocity = wavefields[:, 0:3]
        stress = wavefields[:, 3:9]
        for step_index in range(STEPS):
            velocity = velocity_update(velocity, stress, buoyancy, next_cell(stress[:, 0], 1), prev_cell(stress[:, 3:5], 2))
            stress, strains = stress_update(velocity, stress, lame_lambda, lame_mu, prev_cell(velocity[:, 0:1], 2), next_cell(velocity[:, 1:3], 2))
            lambda_term, shear_term = imaging(strains)
            grad_lambda = grad_lambda + lambda_term
            grad_shear = grad_shear + shear_term
            pushes = jnp.stack([source_spot * source_wavelet[shot_index, step_index], receiver_push[step_index]])
            stress = stress.at[:, 0:3].add(-TIME_STEP * pushes[:, None])
        finals.append(jnp.concatenate([velocity[1], stress[1]], axis=0))
    return jnp.stack(finals), grad_lambda, grad_shear
```

```python
import functools
import jax
import jax.numpy as jnp
from jax import lax
from jax.experimental import pallas as pl
from jax.experimental.pallas import tpu as pltpu
from jax.sharding import PartitionSpec as P

DT = 0.3
MESH = pl.DeviceIdType.MESH
MSG = 16


def at_virtual(shot, slab):
    core, half = lax.rem(shot, 2), lax.rem(slab, 2)
    return (shot - core + half, slab - half + core)


def kernel(
    n_shot,
    n_slab,
    steps,
    lam_hbm,
    mu_hbm,
    buo_hbm,
    fwd_hbm,
    adj_hbm,
    wavelet_ref,
    source_ref,
    traces_ref,
    rslab_ref,
    rcell_ref,
    adj_out,
    lam_out,
    mu_out,
    st,
    par,
    edge,
    edge_par,
    rx_s,
    rx_v,
    tx_s,
    tx_v,
    msg,
    rx_msg,
    push,
    spot,
    amp,
    grad,
    rx_grad,
    in_send,
    in_recv,
    edge_send,
    edge_recv,
    s_send,
    s_recv,
    v_send,
    v_recv,
    msg_send,
    msg_recv,
    grad_send,
    grad_recv,
    out_send,
    out_recv,
):
    ny, nz = st.shape[3], st.shape[4]
    cells = 2 * ny * nz
    rows = 2 * ny
    shot, slab = lax.axis_index("shot"), lax.axis_index("slab")
    my_shot, my_slab = at_virtual(shot, slab)
    stays = lax.rem(shot, 2) == lax.rem(slab, 2)
    moves = jnp.logical_not(stays)
    partner = (my_shot, my_slab)
    prev_dev = at_virtual(my_shot, jnp.maximum(my_slab - 1, 0))
    next_dev = at_virtual(my_shot, jnp.minimum(my_slab + 1, n_slab - 1))
    has_prev, has_next = my_slab > 0, my_slab < n_slab - 1

    def remote(src, dst, ssem, rsem, dev):
        return pltpu.make_async_remote_copy(
            src_ref=src, dst_ref=dst, send_sem=ssem, recv_sem=rsem, device_id=dev, device_id_type=MESH
        )

    msg[...] = jnp.zeros_like(msg)
    msg[0:steps] = traces_ref[0]
    msg[steps : steps + 1] = rslab_ref[...].astype(jnp.float32)
    msg[steps + 1 : steps + 2] = rcell_ref[...].astype(jnp.float32)
    msg[steps + 2 : steps + 3, 0:steps] = wavelet_ref[...]
    msg[steps + 3 : steps + 4] = jnp.broadcast_to(source_ref[...].astype(jnp.float32), (1, 128))

    def msg_copy(t):
        return remote(msg, rx_msg.at[slab], msg_send.at[t], msg_recv.at[slab], at_virtual(shot, t))

    def msg_local():
        return pltpu.make_async_copy(msg, rx_msg.at[slab], msg_recv.at[slab])

    def is_self(t):
        return jnp.logical_and(stays, t == slab)

    def send_msg(t, carry):
        pl.when(jnp.logical_not(is_self(t)))(lambda: msg_copy(t).start())
        return carry

    lax.fori_loop(0, n_slab, send_msg, 0)
    pl.when(stays)(lambda: msg_local().start())

    orig_prev = at_virtual(shot, jnp.maximum(slab - 1, 0))
    orig_next = at_virtual(shot, jnp.minimum(slab + 1, n_slab - 1))
    to_next, to_prev = [], []
    for w, field in enumerate((fwd_hbm, adj_hbm)):
        to_next += [
            (field.at[0, 0, 1], edge.at[w, 0]),
            (field.at[0, 6:8, 1], edge.at[w, 1:3]),
            (field.at[0, 3, 1], rx_s.at[0, 0, w]),
        ]
        to_prev += [(field.at[0, 3, 0], rx_s.at[0, 1, w])]
    to_next += [(mu_hbm.at[1], edge_par.at[0]), (buo_hbm.at[1], edge_par.at[1])]
    next_copies = [
        remote(a, b, edge_send.at[i], edge_recv.at[i], orig_next) for i, (a, b) in enumerate(to_next)
    ]
    prev_copies = [
        remote(a, b, edge_send.at[8 + i], edge_recv.at[8 + i], orig_prev)
        for i, (a, b) in enumerate(to_prev)
    ]
    sends_next, sends_prev = slab < n_slab - 1, slab > 0

    @pl.when(sends_next)
    def _():
        for copy in next_copies:
            copy.start()

    @pl.when(sends_prev)
    def _():
        for copy in prev_copies:
            copy.start()

    pairs = [
        (fwd_hbm.at[0], st.at[0]),
        (adj_hbm.at[0], st.at[1]),
        (lam_hbm, par.at[0]),
        (mu_hbm, par.at[1]),
        (buo_hbm, par.at[2]),
    ]
    local_in = [pltpu.make_async_copy(a, b, in_recv.at[i]) for i, (a, b) in enumerate(pairs)]
    swap_in = [remote(a, b, in_send.at[i], in_recv.at[i], partner) for i, (a, b) in enumerate(pairs)]

    @pl.when(stays)
    def _():
        for copy in local_in:
            copy.start()

    @pl.when(moves)
    def _():
        for copy in swap_in:
            copy.start()

    @pl.when(jnp.logical_not(has_prev))
    def _():
        edge[...] = jnp.zeros_like(edge)
        edge_par[...] = jnp.zeros_like(edge_par)
        rx_s[:, 0] = jnp.zeros((steps, 2, ny, nz), jnp.float32)
        rx_v[:, 0] = jnp.zeros((steps, 2, 2, ny, nz), jnp.float32)

    @pl.when(jnp.logical_not(has_next))
    def _():
        rx_s[:, 1] = jnp.zeros((steps, 2, ny, nz), jnp.float32)
        rx_v[:, 1] = jnp.zeros((steps, 2, 2, ny, nz), jnp.float32)

    grad[...] = jnp.zeros_like(grad)
    push[...] = jnp.zeros_like(push)

    row_of = lax.broadcasted_iota(jnp.int32, (rows, 128), 0)
    col_of = lax.broadcasted_iota(jnp.int32, (nz, 128), 0)

    def scatter(q, carry):
        from_dev = at_virtual(my_shot, q)
        pltpu.make_async_copy(msg, rx_msg.at[q], msg_recv.at[q]).wait()
        block = rx_msg[q]
        named = block[steps : steps + 1].astype(jnp.int32)
        cell = block[steps + 1 : steps + 2].astype(jnp.int32)
        row = jnp.where(named == my_slab, cell // nz, -1)
        hit = row_of == row
        column = (col_of == lax.rem(cell, nz)).astype(jnp.float32).astype(jnp.bfloat16)
        trace = block[0:steps]
        high = trace.astype(jnp.bfloat16).astype(jnp.float32)
        middle = (trace - high).astype(jnp.bfloat16).astype(jnp.float32)
        low = trace - high - middle
        for k in range(steps):
            left = jnp.concatenate(
                [jnp.where(hit, part[k : k + 1], 0.0) for part in (high, middle, low)], axis=0
            ).astype(jnp.bfloat16)
            out = lax.dot_general(
                left, column, (((1,), (1,)), ((), ())), preferred_element_type=jnp.float32
            )
            push[k] += out[0:rows] + out[rows : 2 * rows] + out[2 * rows :]
        return carry

    lax.fori_loop(0, n_slab, scatter, 0)

    head = rx_msg[my_slab]
    source = head[steps + 3 : steps + 4].astype(jnp.int32) - my_slab * cells
    flat = row_of * nz + lax.broadcasted_iota(jnp.int32, (rows, nz), 1)
    spot[...] = (flat == source).astype(jnp.float32)
    for k in range(steps):
        amp[k] = jnp.broadcast_to(DT * head[steps + 2 : steps + 3, k : k + 1], (8, nz))

    @pl.when(stays)
    def _():
        for copy in local_in:
            copy.wait()

    @pl.when(moves)
    def _():
        for copy in swap_in:
            copy.wait_recv()

    @pl.when(has_prev)
    def _():
        for copy in next_copies:
            copy.wait_recv()

    @pl.when(has_next)
    def _():
        for copy in prev_copies:
            copy.wait_recv()

    y_at = lax.broadcasted_iota(jnp.int32, (ny, nz), 0)
    z_at = lax.broadcasted_iota(jnp.int32, (ny, nz), 1)

    def yn(a):
        return jnp.where(y_at < ny - 1, pltpu.roll(a, ny - 1, 0), 0.0)

    def yp(a):
        return jnp.where(y_at > 0, pltpu.roll(a, 1, 0), 0.0)

    def zn(a):
        return jnp.where(z_at < nz - 1, pltpu.roll(a, nz - 1, 1), 0.0)

    def zp(a):
        return jnp.where(z_at > 0, pltpu.roll(a, 1, 1), 0.0)

    par[0] = DT * par[0]
    par[1] = DT * par[1]
    par[2] = DT * par[2]
    edge_par[...] = DT * edge_par[...]

    def v_copies(k):
        return (
            remote(tx_v.at[k, 0], rx_v.at[k, 1], v_send.at[k, 0], v_recv.at[k, 1], prev_dev),
            remote(tx_v.at[k, 1], rx_v.at[k, 0], v_send.at[k, 1], v_recv.at[k, 0], next_dev),
        )

    def s_copies(k):
        return (
            remote(tx_s.at[k, 0], rx_s.at[k, 1], s_send.at[k, 0], s_recv.at[k, 1], prev_dev),
            remote(tx_s.at[k, 1], rx_s.at[k, 0], s_send.at[k, 1], s_recv.at[k, 0], next_dev),
        )

    def step(k, carry):
        for w in range(2):
            for i in range(2):
                sxy0 = edge[w, 1] if i == 0 else st[w, 6, 0]
                sxz0 = edge[w, 2] if i == 0 else st[w, 7, 0]
                syy, szz, syz = st[w, 4, i], st[w, 5, i], st[w, 8, i]
                vy = st[w, 1, i] - par[2, i] * (
                    (st[w, 6, i] - sxy0) + (yn(syy) - syy) + (syz - zp(syz))
                )
                vz = st[w, 2, i] - par[2, i] * (
                    (st[w, 7, i] - sxz0) + (syz - yp(syz)) + (zn(szz) - szz)
                )
                st[w, 1, i] = vy
                st[w, 2, i] = vz
                tx_v[k, i, w, 0] = vy
                tx_v[k, i, w, 1] = vz
        back, ahead = v_copies(k)
        pl.when(has_prev)(lambda: back.start())
        pl.when(has_next)(lambda: ahead.start())

        @pl.when(k > 0)
        def _():
            s_back, s_ahead = s_copies(k)
            pl.when(has_prev)(lambda: s_ahead.wait_recv())
            pl.when(has_next)(lambda: s_back.wait_recv())

        for w in range(2):
            sxx = [rx_s[k, 0, w], st[w, 3, 0], st[w, 3, 1], rx_s[k, 1, w]]
            for i in range(3):
                sxy = edge[w, 1] if i == 0 else st[w, 6, i - 1]
                sxz = edge[w, 2] if i == 0 else st[w, 7, i - 1]
                factor = edge_par[1] if i == 0 else par[2, i - 1]
                change = factor * ((sxx[i + 1] - sxx[i]) + (sxy - yp(sxy)) + (sxz - zp(sxz)))
                if i == 0:
                    edge[w, 0] = edge[w, 0] - change
                else:
                    st[w, 0, i - 1] = st[w, 0, i - 1] - change

        for i in range(2):
            terms = []
            at = pl.ds(i * ny, ny)
            gains = (amp[k, 0:1] * spot[at], DT * push[k, at])
            for w in range(2):
                vx0 = edge[w, 0] if i == 0 else st[w, 0, 0]
                vy, vz = st[w, 1, i], st[w, 2, i]
                exx = st[w, 0, i] - vx0
                eyy = vy - yp(vy)
                ezz = vz - zp(vz)
                tr = exx + eyy + ezz
                common = par[0, i] * tr + gains[w]
                twice = 2.0 * par[1, i]
                sxx = st[w, 3, i] - (common + twice * exx)
                st[w, 3, i] = sxx
                tx_s[k, i, w] = sxx
                st[w, 4, i] = st[w, 4, i] - (common + twice * eyy)
                st[w, 5, i] = st[w, 5, i] - (common + twice * ezz)
                terms.append((exx, eyy, ezz, tr))
            f, a = terms
            grad[0, i] += f[3] * a[3]
            grad[1, i] += 2.0 * (f[0] * a[0] + f[1] * a[1] + f[2] * a[2])

        @pl.when(k < steps - 1)
        def _():
            s_back = remote(
                tx_s.at[k, 0], rx_s.at[k + 1, 1], s_send.at[k, 0], s_recv.at[k + 1, 1], prev_dev
            )
            s_ahead = remote(
                tx_s.at[k, 1], rx_s.at[k + 1, 0], s_send.at[k, 1], s_recv.at[k + 1, 0], next_dev
            )
            pl.when(has_prev)(lambda: s_back.start())
            pl.when(has_next)(lambda: s_ahead.start())

        for i in range(2):
            eyz = []
            for w in range(2):
                vy, vz = st[w, 1, i], st[w, 2, i]
                strain = (zn(vy) - vy) + (yn(vz) - vz)
                st[w, 8, i] = st[w, 8, i] - par[1, i] * strain
                eyz.append(strain)
            grad[1, i] += eyz[0] * eyz[1]

        pl.when(has_prev)(lambda: ahead.wait_recv())
        pl.when(has_next)(lambda: back.wait_recv())
        for i in range(3):
            pair = []
            for w in range(2):
                vx = edge[w, 0] if i == 0 else st[w, 0, i - 1]
                vy0 = rx_v[k, 0, w, 0] if i == 0 else st[w, 1, i - 1]
                vz0 = rx_v[k, 0, w, 1] if i == 0 else st[w, 2, i - 1]
                vy1 = rx_v[k, 1, w, 0] if i == 2 else st[w, 1, i]
                vz1 = rx_v[k, 1, w, 1] if i == 2 else st[w, 2, i]
                exy = (yn(vx) - vx) + (vy1 - vy0)
                exz = (zn(vx) - vx) + (vz1 - vz0)
                if i == 0:
                    edge[w, 1] = edge[w, 1] - edge_par[0] * exy
                    edge[w, 2] = edge[w, 2] - edge_par[0] * exz
                else:
                    st[w, 6, i - 1] = st[w, 6, i - 1] - par[1, i - 1] * exy
                    st[w, 7, i - 1] = st[w, 7, i - 1] - par[1, i - 1] * exz
                pair.append((exy, exz))
            if i > 0:
                grad[1, i - 1] += pair[0][0] * pair[1][0] + pair[0][1] * pair[1][1]
        return carry

    lax.fori_loop(0, steps, step, 0)

    out_local = pltpu.make_async_copy(st.at[1], adj_out.at[0], out_recv)
    out_remote = remote(st.at[1], adj_out.at[0], out_send, out_recv, partner)

    grad[...] = DT * grad[...]
    part = ny // n_shot

    def grad_remote(t):
        return remote(
            grad.at[:, :, pl.ds(t * part, part)],
            rx_grad.at[my_shot],
            grad_send.at[t],
            grad_recv.at[my_shot],
            (jnp.int32(t), my_slab),
        )

    for t in range(n_shot):
        own = jnp.logical_and(stays, t == shot)

        @pl.when(jnp.logical_not(own))
        def _(t=t):
            grad_remote(t).start()

        @pl.when(own)
        def _(t=t):
            rx_grad[t] = grad[:, :, t * part : (t + 1) * part]

    pl.when(stays)(lambda: out_local.start())
    pl.when(moves)(lambda: out_remote.start())

    for t in range(n_shot):
        own = jnp.logical_and(stays, t == shot)

        @pl.when(jnp.logical_not(own))
        def _(t=t):
            remote(
                grad.at[:, :, pl.ds(t * part, part)],
                rx_grad.at[t],
                grad_send.at[t],
                grad_recv.at[t],
                (jnp.int32(t), my_slab),
            ).wait_recv()

    total = rx_grad[0]
    for t in range(1, n_shot):
        total = total + rx_grad[t]
    lam_out[...] = total[0]
    mu_out[...] = total[1]

    for t in range(n_shot):
        own = jnp.logical_and(stays, t == shot)
        pl.when(jnp.logical_not(own))(lambda t=t: grad_remote(t).wait_send())

    def drain(k, carry):
        back, ahead = v_copies(k)
        pl.when(has_prev)(lambda: back.wait_send())
        pl.when(has_next)(lambda: ahead.wait_send())

        @pl.when(k < steps - 1)
        def _():
            s_back, s_ahead = s_copies(k)
            pl.when(has_prev)(lambda: s_back.wait_send())
            pl.when(has_next)(lambda: s_ahead.wait_send())

        return carry

    lax.fori_loop(0, steps, drain, 0)

    def drain_msg(t, carry):
        pl.when(jnp.logical_not(is_self(t)))(lambda: msg_copy(t).wait_send())
        return carry

    lax.fori_loop(0, n_slab, drain_msg, 0)

    @pl.when(sends_next)
    def _():
        for copy in next_copies:
            copy.wait_send()

    @pl.when(sends_prev)
    def _():
        for copy in prev_copies:
            copy.wait_send()

    pl.when(stays)(lambda: out_local.wait())

    @pl.when(moves)
    def _():
        for copy in swap_in:
            copy.wait_send()
        out_remote.wait()


def shards(n_shot, n_slab, lam, mu, buo, fwd, adj, wavelet, source, traces, rslab, rcell):
    planes, ny, nz = lam.shape
    steps = wavelet.shape[1]
    nrec = traces.shape[2]
    f32 = jnp.float32
    vmem = pl.BlockSpec(memory_space=pltpu.VMEM)
    hbm = pl.BlockSpec(memory_space=pl.ANY)
    dma = pltpu.SemaphoreType.DMA
    part = ny // n_shot
    return pl.pallas_call(
        functools.partial(kernel, n_shot, n_slab, steps),
        out_shape=(
            jax.ShapeDtypeStruct((1, 9, planes, ny, nz), f32),
            jax.ShapeDtypeStruct((planes, part, nz), f32),
            jax.ShapeDtypeStruct((planes, part, nz), f32),
        ),
        in_specs=[hbm] * 5 + [vmem] * 5,
        out_specs=(hbm, vmem, vmem),
        scratch_shapes=[
            pltpu.VMEM((2, 9, planes, ny, nz), f32),
            pltpu.VMEM((3, planes, ny, nz), f32),
            pltpu.VMEM((2, 3, ny, nz), f32),
            pltpu.VMEM((2, ny, nz), f32),
            pltpu.VMEM((steps, 2, 2, ny, nz), f32),
            pltpu.VMEM((steps, 2, 2, 2, ny, nz), f32),
            pltpu.VMEM((steps, 2, 2, ny, nz), f32),
            pltpu.VMEM((steps, 2, 2, 2, ny, nz), f32),
            pltpu.VMEM((MSG, nrec), f32),
            pltpu.VMEM((n_slab, MSG, nrec), f32),
            pltpu.VMEM((steps, planes * ny, nz), f32),
            pltpu.VMEM((planes * ny, nz), f32),
            pltpu.VMEM((steps, 8, nz), f32),
            pltpu.VMEM((2, planes, ny, nz), f32),
            pltpu.VMEM((n_shot, 2, planes, part, nz), f32),
            dma((5,)),
            dma((5,)),
            dma((10,)),
            dma((10,)),
            dma((steps, 2)),
            dma((steps, 2)),
            dma((steps, 2)),
            dma((steps, 2)),
            dma((n_slab,)),
            dma((n_slab,)),
            dma((n_shot,)),
            dma((n_shot,)),
            dma,
            dma,
        ],
        compiler_params=pltpu.CompilerParams(
            has_side_effects=True, vmem_limit_bytes=24 * 1024 * 1024
        ),
        cost_estimate=pl.CostEstimate(flops=10**7, bytes_accessed=10**6, transcendentals=0),
    )(
        lam,
        mu,
        buo,
        fwd,
        adj,
        wavelet,
        source.reshape(1, 1),
        traces,
        rslab.reshape(1, nrec),
        rcell.reshape(1, nrec),
    )


def solution(mesh):
    in_specs = (
        P("slab", None, None),
        P("slab", None, None),
        P("slab", None, None),
        P("shot", None, "slab", None, None),
        P("shot", None, "slab", None, None),
        P("shot", None),
        P("shot"),
        P("shot", None, "slab"),
        P("slab", None),
        P("slab"),
    )
    out_specs = (
        P("shot", None, "slab", None, None),
        P("slab", "shot", None),
        P("slab", "shot", None),
    )
    body = functools.partial(shards, mesh.shape["shot"], mesh.shape["slab"])
    return jax.shard_map(body, mesh=mesh, in_specs=in_specs, out_specs=out_specs, check_vma=False)
```

```python
import functools
import jax
import jax.numpy as jnp
from jax import lax
from jax.experimental import pallas as pl
from jax.experimental.pallas import tpu as pltpu
from jax.sharding import PartitionSpec as P

DT = 0.3
MESH = pl.DeviceIdType.MESH
MSG = 16


def at_virtual(shot, slab):
    core, half = lax.rem(shot, 2), lax.rem(slab, 2)
    return (shot - core + half, slab - half + core)


def kernel(
    n_shot,
    n_slab,
    steps,
    lam_hbm,
    mu_hbm,
    buo_hbm,
    fwd_hbm,
    adj_hbm,
    wavelet_hbm,
    source_hbm,
    traces_hbm,
    rslab_hbm,
    rcell_hbm,
    adj_out,
    lam_out,
    mu_out,
    wavelet_ref,
    source_ref,
    traces_ref,
    rslab_ref,
    rcell_ref,
    small_sem,
    st,
    par,
    edge,
    edge_par,
    rx_s,
    rx_v,
    tx_s,
    tx_v,
    msg,
    rx_msg,
    push,
    spot,
    amp,
    grad,
    rx_grad,
    in_send,
    in_recv,
    edge_send,
    edge_recv,
    s_send,
    s_recv,
    v_send,
    v_recv,
    msg_send,
    msg_recv,
    grad_send,
    grad_recv,
    out_send,
    out_recv,
):
    ny, nz = st.shape[3], st.shape[4]
    cells = 2 * ny * nz
    rows = 2 * ny
    shot, slab = lax.axis_index("shot"), lax.axis_index("slab")
    my_shot, my_slab = at_virtual(shot, slab)
    stays = lax.rem(shot, 2) == lax.rem(slab, 2)
    moves = jnp.logical_not(stays)
    partner = (my_shot, my_slab)
    prev_dev = at_virtual(my_shot, jnp.maximum(my_slab - 1, 0))
    next_dev = at_virtual(my_shot, jnp.minimum(my_slab + 1, n_slab - 1))
    has_prev, has_next = my_slab > 0, my_slab < n_slab - 1

    def remote(src, dst, ssem, rsem, dev):
        return pltpu.make_async_remote_copy(
            src_ref=src, dst_ref=dst, send_sem=ssem, recv_sem=rsem, device_id=dev, device_id_type=MESH
        )

    small = [
        pltpu.make_async_copy(a, b, small_sem.at[i])
        for i, (a, b) in enumerate(
            (
                (wavelet_hbm, wavelet_ref),
                (source_hbm, source_ref),
                (traces_hbm, traces_ref),
                (rslab_hbm, rslab_ref),
                (rcell_hbm, rcell_ref),
            )
        )
    ]
    for copy in small:
        copy.start()
    msg[...] = jnp.zeros_like(msg)
    for copy in small:
        copy.wait()
    msg[0:steps] = traces_ref[0]
    msg[steps : steps + 1] = rslab_ref[...].astype(jnp.float32)
    msg[steps + 1 : steps + 2] = rcell_ref[...].astype(jnp.float32)
    msg[steps + 2 : steps + 3, 0:steps] = wavelet_ref[...]
    msg[steps + 3 : steps + 4] = jnp.full((1, msg.shape[1]), source_ref[0], jnp.int32).astype(
        jnp.float32
    )

    def msg_copy(t):
        return remote(msg, rx_msg.at[slab], msg_send.at[t], msg_recv.at[slab], at_virtual(shot, t))

    def msg_local():
        return pltpu.make_async_copy(msg, rx_msg.at[slab], msg_recv.at[slab])

    def is_self(t):
        return jnp.logical_and(stays, t == slab)

    def send_msg(t, carry):
        pl.when(jnp.logical_not(is_self(t)))(lambda: msg_copy(t).start())
        return carry

    lax.fori_loop(0, n_slab, send_msg, 0)
    pl.when(stays)(lambda: msg_local().start())

    orig_prev = at_virtual(shot, jnp.maximum(slab - 1, 0))
    orig_next = at_virtual(shot, jnp.minimum(slab + 1, n_slab - 1))
    to_next, to_prev = [], []
    for w, field in enumerate((fwd_hbm, adj_hbm)):
        to_next += [
            (field.at[0, 0, 1], edge.at[w, 0]),
            (field.at[0, 6:8, 1], edge.at[w, 1:3]),
            (field.at[0, 3, 1], rx_s.at[0, 0, w]),
        ]
        to_prev += [(field.at[0, 3, 0], rx_s.at[0, 1, w])]
    to_next += [(mu_hbm.at[1], edge_par.at[0]), (buo_hbm.at[1], edge_par.at[1])]
    next_copies = [
        remote(a, b, edge_send.at[i], edge_recv.at[i], orig_next) for i, (a, b) in enumerate(to_next)
    ]
    prev_copies = [
        remote(a, b, edge_send.at[8 + i], edge_recv.at[8 + i], orig_prev)
        for i, (a, b) in enumerate(to_prev)
    ]
    sends_next, sends_prev = slab < n_slab - 1, slab > 0

    @pl.when(sends_next)
    def _():
        for copy in next_copies:
            copy.start()

    @pl.when(sends_prev)
    def _():
        for copy in prev_copies:
            copy.start()

    pairs = [
        (fwd_hbm.at[0], st.at[0]),
        (adj_hbm.at[0], st.at[1]),
        (lam_hbm, par.at[0]),
        (mu_hbm, par.at[1]),
        (buo_hbm, par.at[2]),
    ]
    local_in = [pltpu.make_async_copy(a, b, in_recv.at[i]) for i, (a, b) in enumerate(pairs)]
    swap_in = [remote(a, b, in_send.at[i], in_recv.at[i], partner) for i, (a, b) in enumerate(pairs)]

    @pl.when(stays)
    def _():
        for copy in local_in:
            copy.start()

    @pl.when(moves)
    def _():
        for copy in swap_in:
            copy.start()

    @pl.when(jnp.logical_not(has_prev))
    def _():
        edge[...] = jnp.zeros_like(edge)
        edge_par[...] = jnp.zeros_like(edge_par)
        rx_s[:, 0] = jnp.zeros((steps, 2, ny, nz), jnp.float32)
        rx_v[:, 0] = jnp.zeros((steps, 2, 2, ny, nz), jnp.float32)

    @pl.when(jnp.logical_not(has_next))
    def _():
        rx_s[:, 1] = jnp.zeros((steps, 2, ny, nz), jnp.float32)
        rx_v[:, 1] = jnp.zeros((steps, 2, 2, ny, nz), jnp.float32)

    grad[...] = jnp.zeros_like(grad)
    push[...] = jnp.zeros_like(push)

    nrec = msg.shape[1]
    row_of = lax.broadcasted_iota(jnp.int32, (rows, nrec), 0)
    col_of = lax.broadcasted_iota(jnp.int32, (nz, nrec), 0)

    def scatter(pair, carry):
        left, right = [], []
        for q in (2 * pair, 2 * pair + 1):
            pltpu.make_async_copy(msg, rx_msg.at[q], msg_recv.at[q]).wait()
            block = rx_msg[q]
            named = block[steps : steps + 1].astype(jnp.int32)
            cell = block[steps + 1 : steps + 2].astype(jnp.int32)
            row = jnp.where(named == my_slab, cell // nz, -1)
            hit = row_of == row
            column = (col_of == lax.rem(cell, nz)).astype(jnp.float32).astype(jnp.bfloat16)
            trace = block[0:steps]
            high = trace.astype(jnp.bfloat16).astype(jnp.float32)
            low = trace - high
            left.append(
                jnp.concatenate(
                    [
                        jnp.where(hit, term[k : k + 1], 0.0).astype(jnp.bfloat16)
                        for term in (high, low)
                        for k in range(steps)
                    ],
                    axis=0,
                )
            )
            right.append(column)
        out = lax.dot_general(
            jnp.concatenate(left, axis=1),
            jnp.concatenate(right, axis=1),
            (((1,), (1,)), ((), ())),
            preferred_element_type=jnp.float32,
        )
        for k in range(steps):
            push[k] += out[k * rows : (k + 1) * rows] + out[(steps + k) * rows : (steps + k + 1) * rows]
        return carry

    lax.fori_loop(0, n_slab // 2, scatter, 0)

    head = rx_msg[my_slab]
    source = head[steps + 3 : steps + 4].astype(jnp.int32) - my_slab * cells
    flat = lax.broadcasted_iota(jnp.int32, (rows, nz), 0) * nz
    flat = flat + lax.broadcasted_iota(jnp.int32, (rows, nz), 1)
    spot[...] = (flat == source).astype(jnp.float32)
    for k in range(steps):
        amp[k] = jnp.broadcast_to(DT * head[steps + 2 : steps + 3, k : k + 1], (8, nz))

    @pl.when(stays)
    def _():
        for copy in local_in:
            copy.wait()

    @pl.when(moves)
    def _():
        for copy in swap_in:
            copy.wait_recv()

    @pl.when(has_prev)
    def _():
        for copy in next_copies:
            copy.wait_recv()

    @pl.when(has_next)
    def _():
        for copy in prev_copies:
            copy.wait_recv()

    y_at = lax.broadcasted_iota(jnp.int32, (ny, nz), 0)
    z_at = lax.broadcasted_iota(jnp.int32, (ny, nz), 1)

    def yn(a):
        return jnp.where(y_at < ny - 1, pltpu.roll(a, ny - 1, 0), 0.0)

    def yp(a):
        return jnp.where(y_at > 0, pltpu.roll(a, 1, 0), 0.0)

    def zn(a):
        return jnp.where(z_at < nz - 1, pltpu.roll(a, nz - 1, 1), 0.0)

    def zp(a):
        return jnp.where(z_at > 0, pltpu.roll(a, 1, 1), 0.0)

    par[0] = DT * par[0]
    par[1] = DT * par[1]
    par[2] = DT * par[2]
    edge_par[...] = DT * edge_par[...]

    def v_copies(k):
        return (
            remote(tx_v.at[k, 0], rx_v.at[k, 1], v_send.at[k, 0], v_recv.at[k, 1], prev_dev),
            remote(tx_v.at[k, 1], rx_v.at[k, 0], v_send.at[k, 1], v_recv.at[k, 0], next_dev),
        )

    def s_copies(k):
        return (
            remote(tx_s.at[k, 0], rx_s.at[k, 1], s_send.at[k, 0], s_recv.at[k, 1], prev_dev),
            remote(tx_s.at[k, 1], rx_s.at[k, 0], s_send.at[k, 1], s_recv.at[k, 0], next_dev),
        )

    groups = ((0, 3), (3, 6), (8, 9), (6, 8))

    def home_local(n):
        a, b = groups[n]
        return pltpu.make_async_copy(st.at[1, a:b], adj_out.at[0, a:b], out_recv.at[n])

    def home_away(n):
        a, b = groups[n]
        return remote(st.at[1, a:b], adj_out.at[0, a:b], out_send.at[n], out_recv.at[n], partner)

    def go_home(n):
        pl.when(stays)(lambda: home_local(n).start())
        pl.when(moves)(lambda: home_away(n).start())

    def step(k, carry):
        for w in range(2):
            for i in range(2):
                sxy0 = edge[w, 1] if i == 0 else st[w, 6, 0]
                sxz0 = edge[w, 2] if i == 0 else st[w, 7, 0]
                syy, szz, syz = st[w, 4, i], st[w, 5, i], st[w, 8, i]
                vy = st[w, 1, i] - par[2, i] * (
                    (st[w, 6, i] - sxy0) + (yn(syy) - syy) + (syz - zp(syz))
                )
                vz = st[w, 2, i] - par[2, i] * (
                    (st[w, 7, i] - sxz0) + (syz - yp(syz)) + (zn(szz) - szz)
                )
                st[w, 1, i] = vy
                st[w, 2, i] = vz
                tx_v[k, i, w, 0] = vy
                tx_v[k, i, w, 1] = vz
        back, ahead = v_copies(k)
        pl.when(has_prev)(lambda: back.start())
        pl.when(has_next)(lambda: ahead.start())

        @pl.when(k > 0)
        def _():
            s_back, s_ahead = s_copies(k)
            pl.when(has_prev)(lambda: s_ahead.wait_recv())
            pl.when(has_next)(lambda: s_back.wait_recv())

        for w in range(2):
            sxx = [rx_s[k, 0, w], st[w, 3, 0], st[w, 3, 1], rx_s[k, 1, w]]
            for i in range(3):
                sxy = edge[w, 1] if i == 0 else st[w, 6, i - 1]
                sxz = edge[w, 2] if i == 0 else st[w, 7, i - 1]
                factor = edge_par[1] if i == 0 else par[2, i - 1]
                change = factor * ((sxx[i + 1] - sxx[i]) + (sxy - yp(sxy)) + (sxz - zp(sxz)))
                if i == 0:
                    edge[w, 0] = edge[w, 0] - change
                else:
                    st[w, 0, i - 1] = st[w, 0, i - 1] - change

        pl.when(k == steps - 1)(lambda: go_home(0))

        for i in range(2):
            terms = []
            at = pl.ds(i * ny, ny)
            gains = (amp[k, 0:1] * spot[at], DT * push[k, at])
            for w in range(2):
                vx0 = edge[w, 0] if i == 0 else st[w, 0, 0]
                vy, vz = st[w, 1, i], st[w, 2, i]
                exx = st[w, 0, i] - vx0
                eyy = vy - yp(vy)
                ezz = vz - zp(vz)
                tr = exx + eyy + ezz
                common = par[0, i] * tr + gains[w]
                twice = 2.0 * par[1, i]
                sxx = st[w, 3, i] - (common + twice * exx)
                st[w, 3, i] = sxx
                tx_s[k, i, w] = sxx
                st[w, 4, i] = st[w, 4, i] - (common + twice * eyy)
                st[w, 5, i] = st[w, 5, i] - (common + twice * ezz)
                terms.append((exx, eyy, ezz, tr))
            f, a = terms
            grad[0, i] += f[3] * a[3]
            grad[1, i] += 2.0 * (f[0] * a[0] + f[1] * a[1] + f[2] * a[2])

        @pl.when(k < steps - 1)
        def _():
            s_back = remote(
                tx_s.at[k, 0], rx_s.at[k + 1, 1], s_send.at[k, 0], s_recv.at[k + 1, 1], prev_dev
            )
            s_ahead = remote(
                tx_s.at[k, 1], rx_s.at[k + 1, 0], s_send.at[k, 1], s_recv.at[k + 1, 0], next_dev
            )
            pl.when(has_prev)(lambda: s_back.start())
            pl.when(has_next)(lambda: s_ahead.start())

        pl.when(k == steps - 1)(lambda: go_home(1))

        for i in range(2):
            eyz = []
            for w in range(2):
                vy, vz = st[w, 1, i], st[w, 2, i]
                strain = (zn(vy) - vy) + (yn(vz) - vz)
                st[w, 8, i] = st[w, 8, i] - par[1, i] * strain
                eyz.append(strain)
            grad[1, i] += eyz[0] * eyz[1]

        pl.when(k == steps - 1)(lambda: go_home(2))

        pl.when(has_prev)(lambda: ahead.wait_recv())
        pl.when(has_next)(lambda: back.wait_recv())
        for i in range(3):
            pair = []
            for w in range(2):
                vx = edge[w, 0] if i == 0 else st[w, 0, i - 1]
                vy0 = rx_v[k, 0, w, 0] if i == 0 else st[w, 1, i - 1]
                vz0 = rx_v[k, 0, w, 1] if i == 0 else st[w, 2, i - 1]
                vy1 = rx_v[k, 1, w, 0] if i == 2 else st[w, 1, i]
                vz1 = rx_v[k, 1, w, 1] if i == 2 else st[w, 2, i]
                exy = (yn(vx) - vx) + (vy1 - vy0)
                exz = (zn(vx) - vx) + (vz1 - vz0)
                if i == 0:
                    edge[w, 1] = edge[w, 1] - edge_par[0] * exy
                    edge[w, 2] = edge[w, 2] - edge_par[0] * exz
                else:
                    st[w, 6, i - 1] = st[w, 6, i - 1] - par[1, i - 1] * exy
                    st[w, 7, i - 1] = st[w, 7, i - 1] - par[1, i - 1] * exz
                pair.append((exy, exz))
            if i > 0:
                grad[1, i - 1] += pair[0][0] * pair[1][0] + pair[0][1] * pair[1][1]
        return carry

    lax.fori_loop(0, steps, step, 0)

    go_home(3)
    grad[...] = DT * grad[...]
    part = ny // n_shot

    def grad_remote(t):
        return remote(
            grad.at[:, :, pl.ds(t * part, part)],
            rx_grad.at[my_shot],
            grad_send.at[t],
            grad_recv.at[my_shot],
            (jnp.int32(t), my_slab),
        )

    for t in range(n_shot):
        own = jnp.logical_and(stays, t == shot)

        @pl.when(jnp.logical_not(own))
        def _(t=t):
            grad_remote(t).start()

        @pl.when(own)
        def _(t=t):
            rx_grad[t] = grad[:, :, t * part : (t + 1) * part]

    for t in range(n_shot):
        own = jnp.logical_and(stays, t == shot)

        @pl.when(jnp.logical_not(own))
        def _(t=t):
            remote(
                grad.at[:, :, pl.ds(t * part, part)],
                rx_grad.at[t],
                grad_send.at[t],
                grad_recv.at[t],
                (jnp.int32(t), my_slab),
            ).wait_recv()

    total = rx_grad[0]
    for t in range(1, n_shot):
        total = total + rx_grad[t]
    lam_out[...] = total[0]
    mu_out[...] = total[1]

    for t in range(n_shot):
        own = jnp.logical_and(stays, t == shot)
        pl.when(jnp.logical_not(own))(lambda t=t: grad_remote(t).wait_send())

    def drain(k, carry):
        back, ahead = v_copies(k)
        pl.when(has_prev)(lambda: back.wait_send())
        pl.when(has_next)(lambda: ahead.wait_send())

        @pl.when(k < steps - 1)
        def _():
            s_back, s_ahead = s_copies(k)
            pl.when(has_prev)(lambda: s_back.wait_send())
            pl.when(has_next)(lambda: s_ahead.wait_send())

        return carry

    lax.fori_loop(0, steps, drain, 0)

    def drain_msg(t, carry):
        pl.when(jnp.logical_not(is_self(t)))(lambda: msg_copy(t).wait_send())
        return carry

    lax.fori_loop(0, n_slab, drain_msg, 0)

    @pl.when(sends_next)
    def _():
        for copy in next_copies:
            copy.wait_send()

    @pl.when(sends_prev)
    def _():
        for copy in prev_copies:
            copy.wait_send()

    @pl.when(stays)
    def _():
        for n in range(len(groups)):
            home_local(n).wait()

    @pl.when(moves)
    def _():
        for copy in swap_in:
            copy.wait_send()
        for n in range(len(groups)):
            home_away(n).wait()


def deliver(a, b, c, a_out, b_out, c_out, sem):
    copies = [
        pltpu.make_async_copy(src, dst, sem.at[i])
        for i, (src, dst) in enumerate(((a, a_out), (b, b_out), (c, c_out)))
    ]
    for copy in copies:
        copy.start()
    for copy in copies:
        copy.wait()


def shards(n_shot, n_slab, lam, mu, buo, fwd, adj, wavelet, source, traces, rslab, rcell):
    planes, ny, nz = lam.shape
    steps = wavelet.shape[1]
    nrec = traces.shape[2]
    f32 = jnp.float32
    vmem = pl.BlockSpec(memory_space=pltpu.VMEM)
    hbm = pl.BlockSpec(memory_space=pl.ANY)
    dma = pltpu.SemaphoreType.DMA
    part = ny // n_shot
    outs = pl.pallas_call(
        functools.partial(kernel, n_shot, n_slab, steps),
        out_shape=(
            jax.ShapeDtypeStruct((1, 9, planes, ny, nz), f32),
            jax.ShapeDtypeStruct((planes, part, nz), f32),
            jax.ShapeDtypeStruct((planes, part, nz), f32),
        ),
        in_specs=[hbm] * 10,
        out_specs=(hbm, vmem, vmem),
        scratch_shapes=[
            pltpu.VMEM((1, steps), f32),
            pltpu.SMEM((1,), jnp.int32),
            pltpu.VMEM((1, steps, nrec), f32),
            pltpu.VMEM((1, nrec), jnp.int32),
            pltpu.VMEM((1, nrec), jnp.int32),
            dma((5,)),
            pltpu.VMEM((2, 9, planes, ny, nz), f32),
            pltpu.VMEM((3, planes, ny, nz), f32),
            pltpu.VMEM((2, 3, ny, nz), f32),
            pltpu.VMEM((2, ny, nz), f32),
            pltpu.VMEM((steps, 2, 2, ny, nz), f32),
            pltpu.VMEM((steps, 2, 2, 2, ny, nz), f32),
            pltpu.VMEM((steps, 2, 2, ny, nz), f32),
            pltpu.VMEM((steps, 2, 2, 2, ny, nz), f32),
            pltpu.VMEM((MSG, nrec), f32),
            pltpu.VMEM((n_slab, MSG, nrec), f32),
            pltpu.VMEM((steps, planes * ny, nz), f32),
            pltpu.VMEM((planes * ny, nz), f32),
            pltpu.VMEM((steps, 8, nz), f32),
            pltpu.VMEM((2, planes, ny, nz), f32),
            pltpu.VMEM((n_shot, 2, planes, part, nz), f32),
            dma((5,)),
            dma((5,)),
            dma((10,)),
            dma((10,)),
            dma((steps, 2)),
            dma((steps, 2)),
            dma((steps, 2)),
            dma((steps, 2)),
            dma((n_slab,)),
            dma((n_slab,)),
            dma((n_shot,)),
            dma((n_shot,)),
            dma((4,)),
            dma((4,)),
        ],
        compiler_params=pltpu.CompilerParams(
            has_side_effects=True, vmem_limit_bytes=60 * 1024 * 1024
        ),
        cost_estimate=pl.CostEstimate(flops=10**7, bytes_accessed=10**6, transcendentals=0),
    )(
        lam,
        mu,
        buo,
        fwd,
        adj,
        wavelet,
        source,
        traces,
        rslab.reshape(1, nrec),
        rcell.reshape(1, nrec),
    )
    return pl.pallas_call(
        deliver,
        out_shape=tuple(jax.ShapeDtypeStruct(o.shape, o.dtype) for o in outs),
        in_specs=[hbm] * 3,
        out_specs=(hbm,) * 3,
        scratch_shapes=[dma((3,))],
        compiler_params=pltpu.CompilerParams(vmem_limit_bytes=60 * 1024 * 1024),
        cost_estimate=pl.CostEstimate(flops=0, bytes_accessed=10**6, transcendentals=0),
    )(*outs)


def solution(mesh):
    in_specs = (
        P("slab", None, None),
        P("slab", None, None),
        P("slab", None, None),
        P("shot", None, "slab", None, None),
        P("shot", None, "slab", None, None),
        P("shot", None),
        P("shot"),
        P("shot", None, "slab"),
        P("slab", None),
        P("slab"),
    )
    out_specs = (
        P("shot", None, "slab", None, None),
        P("slab", "shot", None),
        P("slab", "shot", None),
    )
    body = functools.partial(shards, mesh.shape["shot"], mesh.shape["slab"])
    return jax.shard_map(body, mesh=mesh, in_specs=in_specs, out_specs=out_specs, check_vma=False)
```

```python
import functools
import jax
import jax.numpy as jnp
from jax import lax
from jax.experimental import pallas as pl
from jax.experimental.pallas import tpu as pltpu
from jax.sharding import PartitionSpec as P

DT = 0.3
MESH = pl.DeviceIdType.MESH
MSG = 16


def at_virtual(shot, slab):
    core, half = lax.rem(shot, 2), lax.rem(slab, 2)
    return (shot - core + half, slab - half + core)


def kernel(
    n_shot,
    n_slab,
    steps,
    lam_hbm,
    mu_hbm,
    buo_hbm,
    fwd_hbm,
    adj_hbm,
    wavelet_hbm,
    source_hbm,
    traces_hbm,
    rslab_hbm,
    rcell_hbm,
    adj_out,
    lam_out,
    mu_out,
    wavelet_ref,
    source_ref,
    traces_ref,
    rslab_ref,
    rcell_ref,
    small_sem,
    st,
    par,
    edge,
    edge_par,
    rx_s,
    rx_v,
    tx_s,
    tx_v,
    msg,
    rx_msg,
    push,
    spot,
    amp,
    grad,
    rx_grad,
    own,
    own_par,
    home,
    own_sem,
    swap_recv,
    home_sem,
    in_send,
    in_recv,
    edge_send,
    edge_recv,
    s_send,
    s_recv,
    v_send,
    v_recv,
    msg_send,
    msg_recv,
    grad_send,
    grad_recv,
    out_send,
    out_recv,
):
    ny, nz = st.shape[3], st.shape[4]
    cells = 2 * ny * nz
    rows = 2 * ny
    shot, slab = lax.axis_index("shot"), lax.axis_index("slab")
    my_shot, my_slab = at_virtual(shot, slab)
    stays = lax.rem(shot, 2) == lax.rem(slab, 2)
    moves = jnp.logical_not(stays)
    partner = (my_shot, my_slab)
    prev_dev = at_virtual(my_shot, jnp.maximum(my_slab - 1, 0))
    next_dev = at_virtual(my_shot, jnp.minimum(my_slab + 1, n_slab - 1))
    has_prev, has_next = my_slab > 0, my_slab < n_slab - 1

    def remote(src, dst, ssem, rsem, dev):
        return pltpu.make_async_remote_copy(
            src_ref=src, dst_ref=dst, send_sem=ssem, recv_sem=rsem, device_id=dev, device_id_type=MESH
        )

    small = [
        pltpu.make_async_copy(a, b, small_sem.at[i])
        for i, (a, b) in enumerate(
            (
                (wavelet_hbm, wavelet_ref),
                (source_hbm, source_ref),
                (traces_hbm, traces_ref),
                (rslab_hbm, rslab_ref),
                (rcell_hbm, rcell_ref),
            )
        )
    ]
    for copy in small:
        copy.start()
    own_pairs = [
        (fwd_hbm.at[0], own.at[0]),
        (adj_hbm.at[0], own.at[1]),
        (lam_hbm, own_par.at[0]),
        (mu_hbm, own_par.at[1]),
        (buo_hbm, own_par.at[2]),
    ]
    own_in = [pltpu.make_async_copy(a, b, own_sem.at[i]) for i, (a, b) in enumerate(own_pairs)]
    for copy in own_in:
        copy.start()
    work_pairs = [
        (fwd_hbm.at[0], st.at[0]),
        (adj_hbm.at[0], st.at[1]),
        (lam_hbm, par.at[0]),
        (mu_hbm, par.at[1]),
        (buo_hbm, par.at[2]),
    ]
    local_in = [pltpu.make_async_copy(a, b, in_recv.at[i]) for i, (a, b) in enumerate(work_pairs)]

    @pl.when(stays)
    def _():
        for copy in local_in:
            copy.start()

    first_shot, first_slab = shot - lax.rem(shot, 2), slab - lax.rem(slab, 2)
    barrier = pltpu.get_barrier_semaphore()

    def greet(q, carry):
        for core in range(2):
            me = jnp.logical_and(q == slab, first_shot + core == shot)

            @pl.when(jnp.logical_not(me))
            def _(core=core):
                pl.semaphore_signal(
                    barrier, inc=1, device_id=(first_shot + core, q), device_id_type=MESH
                )

        return carry

    lax.fori_loop(0, n_slab, greet, 0)
    for other in range(0, n_shot, 2):

        @pl.when(first_shot != other)
        def _(other=other):
            for t in (other, other + 1):
                for half in range(2):
                    pl.semaphore_signal(
                        barrier,
                        inc=1,
                        device_id=(jnp.int32(t), first_slab + half),
                        device_id_type=MESH,
                    )

    msg[...] = jnp.zeros_like(msg)
    for copy in small:
        copy.wait()
    msg[0:steps] = traces_ref[0]
    msg[steps : steps + 1] = rslab_ref[...].astype(jnp.float32)
    msg[steps + 1 : steps + 2] = rcell_ref[...].astype(jnp.float32)
    msg[steps + 2 : steps + 3, 0:steps] = wavelet_ref[...]
    msg[steps + 3 : steps + 4] = jnp.full((1, msg.shape[1]), source_ref[0], jnp.int32).astype(
        jnp.float32
    )

    pl.semaphore_wait(barrier, 2 * n_slab - 1 + 2 * (n_shot - 2))

    def msg_copy(t):
        return remote(msg, rx_msg.at[slab], msg_send.at[t], msg_recv.at[slab], at_virtual(shot, t))

    def msg_local():
        return pltpu.make_async_copy(msg, rx_msg.at[slab], msg_recv.at[slab])

    def is_self(t):
        return jnp.logical_and(stays, t == slab)

    def send_msg(t, carry):
        pl.when(jnp.logical_not(is_self(t)))(lambda: msg_copy(t).start())
        return carry

    lax.fori_loop(0, n_slab, send_msg, 0)
    pl.when(stays)(lambda: msg_local().start())

    orig_prev = at_virtual(shot, jnp.maximum(slab - 1, 0))
    orig_next = at_virtual(shot, jnp.minimum(slab + 1, n_slab - 1))
    to_next, to_prev = [], []
    for w in range(2):
        to_next += [
            (own.at[w, 0, 1], edge.at[w, 0]),
            (own.at[w, 6:8, 1], edge.at[w, 1:3]),
            (own.at[w, 3, 1], rx_s.at[0, 0, w]),
        ]
        to_prev += [(own.at[w, 3, 0], rx_s.at[0, 1, w])]
    to_next += [(own_par.at[1, 1], edge_par.at[0]), (own_par.at[2, 1], edge_par.at[1])]
    next_copies = [
        remote(a, b, edge_send.at[i], edge_recv.at[i], orig_next) for i, (a, b) in enumerate(to_next)
    ]
    prev_copies = [
        remote(a, b, edge_send.at[8 + i], edge_recv.at[8 + i], orig_prev)
        for i, (a, b) in enumerate(to_prev)
    ]
    sends_next, sends_prev = slab < n_slab - 1, slab > 0
    for copy in own_in:
        copy.wait()

    @pl.when(sends_next)
    def _():
        for copy in next_copies:
            copy.start()

    @pl.when(sends_prev)
    def _():
        for copy in prev_copies:
            copy.start()

    swap_pairs = [(own.at[w, a : a + 3], st.at[w, a : a + 3]) for a in (0, 3, 6) for w in range(2)]
    swap_pairs += [(own_par, par)]
    swap_in = [
        remote(a, b, in_send.at[i], swap_recv.at[i], partner) for i, (a, b) in enumerate(swap_pairs)
    ]

    @pl.when(moves)
    def _():
        for copy in swap_in:
            copy.start()

    @pl.when(jnp.logical_not(has_prev))
    def _():
        edge[...] = jnp.zeros_like(edge)
        edge_par[...] = jnp.zeros_like(edge_par)
        rx_s[:, 0] = jnp.zeros((steps, 2, ny, nz), jnp.float32)
        rx_v[:, 0] = jnp.zeros((steps, 2, 2, ny, nz), jnp.float32)

    @pl.when(jnp.logical_not(has_next))
    def _():
        rx_s[:, 1] = jnp.zeros((steps, 2, ny, nz), jnp.float32)
        rx_v[:, 1] = jnp.zeros((steps, 2, 2, ny, nz), jnp.float32)

    grad[...] = jnp.zeros_like(grad)
    push[...] = jnp.zeros_like(push)

    nrec = msg.shape[1]
    row_of = lax.broadcasted_iota(jnp.int32, (rows, nrec), 0)
    col_of = lax.broadcasted_iota(jnp.int32, (nz, nrec), 0)

    def scatter(pair, carry):
        left, right = [], []
        for q in (2 * pair, 2 * pair + 1):
            pltpu.make_async_copy(msg, rx_msg.at[q], msg_recv.at[q]).wait()
            block = rx_msg[q]
            named = block[steps : steps + 1].astype(jnp.int32)
            cell = block[steps + 1 : steps + 2].astype(jnp.int32)
            row = jnp.where(named == my_slab, cell // nz, -1)
            hit = row_of == row
            column = (col_of == lax.rem(cell, nz)).astype(jnp.float32).astype(jnp.bfloat16)
            trace = block[0:steps]
            high = trace.astype(jnp.bfloat16).astype(jnp.float32)
            low = trace - high
            left.append(
                jnp.concatenate(
                    [
                        jnp.where(hit, term[k : k + 1], 0.0).astype(jnp.bfloat16)
                        for term in (high, low)
                        for k in range(steps)
                    ],
                    axis=0,
                )
            )
            right.append(column)
        out = lax.dot_general(
            jnp.concatenate(left, axis=1),
            jnp.concatenate(right, axis=1),
            (((1,), (1,)), ((), ())),
            preferred_element_type=jnp.float32,
        )
        for k in range(steps):
            push[k] += out[k * rows : (k + 1) * rows] + out[(steps + k) * rows : (steps + k + 1) * rows]
        return carry

    lax.fori_loop(0, n_slab // 2, scatter, 0)

    head = rx_msg[my_slab]
    source = head[steps + 3 : steps + 4].astype(jnp.int32) - my_slab * cells
    flat = lax.broadcasted_iota(jnp.int32, (rows, nz), 0) * nz
    flat = flat + lax.broadcasted_iota(jnp.int32, (rows, nz), 1)
    spot[...] = (flat == source).astype(jnp.float32)
    for k in range(steps):
        amp[k] = jnp.broadcast_to(DT * head[steps + 2 : steps + 3, k : k + 1], (8, nz))

    @pl.when(stays)
    def _():
        for copy in local_in:
            copy.wait()

    @pl.when(moves)
    def _():
        for copy in swap_in:
            copy.wait_recv()

    @pl.when(has_prev)
    def _():
        for copy in next_copies:
            copy.wait_recv()

    @pl.when(has_next)
    def _():
        for copy in prev_copies:
            copy.wait_recv()

    y_at = lax.broadcasted_iota(jnp.int32, (ny, nz), 0)
    z_at = lax.broadcasted_iota(jnp.int32, (ny, nz), 1)

    def yn(a):
        return jnp.where(y_at < ny - 1, pltpu.roll(a, ny - 1, 0), 0.0)

    def yp(a):
        return jnp.where(y_at > 0, pltpu.roll(a, 1, 0), 0.0)

    def zn(a):
        return jnp.where(z_at < nz - 1, pltpu.roll(a, nz - 1, 1), 0.0)

    def zp(a):
        return jnp.where(z_at > 0, pltpu.roll(a, 1, 1), 0.0)

    par[0] = DT * par[0]
    par[1] = DT * par[1]
    par[2] = DT * par[2]
    edge_par[...] = DT * edge_par[...]

    def v_copies(k):
        return (
            remote(tx_v.at[k, 0], rx_v.at[k, 1], v_send.at[k, 0], v_recv.at[k, 1], prev_dev),
            remote(tx_v.at[k, 1], rx_v.at[k, 0], v_send.at[k, 1], v_recv.at[k, 0], next_dev),
        )

    def s_copies(k):
        return (
            remote(tx_s.at[k, 0], rx_s.at[k, 1], s_send.at[k, 0], s_recv.at[k, 1], prev_dev),
            remote(tx_s.at[k, 1], rx_s.at[k, 0], s_send.at[k, 1], s_recv.at[k, 0], next_dev),
        )

    groups = ((0, 3), (3, 6), (8, 9), (6, 8))

    def home_local(n):
        a, b = groups[n]
        return pltpu.make_async_copy(st.at[1, a:b], adj_out.at[0, a:b], home_sem.at[n])

    def home_land(n):
        a, b = groups[n]
        return pltpu.make_async_copy(home.at[a:b], adj_out.at[0, a:b], home_sem.at[n])

    def home_away(n):
        a, b = groups[n]
        return remote(st.at[1, a:b], home.at[a:b], out_send.at[n], out_recv.at[n], partner)

    def go_home(n):
        pl.when(stays)(lambda: home_local(n).start())
        pl.when(moves)(lambda: home_away(n).start())

    def step(k, carry):
        for w in range(2):
            for i in range(2):
                sxy0 = edge[w, 1] if i == 0 else st[w, 6, 0]
                sxz0 = edge[w, 2] if i == 0 else st[w, 7, 0]
                syy, szz, syz = st[w, 4, i], st[w, 5, i], st[w, 8, i]
                vy = st[w, 1, i] - par[2, i] * (
                    (st[w, 6, i] - sxy0) + (yn(syy) - syy) + (syz - zp(syz))
                )
                vz = st[w, 2, i] - par[2, i] * (
                    (st[w, 7, i] - sxz0) + (syz - yp(syz)) + (zn(szz) - szz)
                )
                st[w, 1, i] = vy
                st[w, 2, i] = vz
                tx_v[k, i, w, 0] = vy
                tx_v[k, i, w, 1] = vz
        back, ahead = v_copies(k)
        pl.when(has_prev)(lambda: back.start())
        pl.when(has_next)(lambda: ahead.start())

        @pl.when(k > 0)
        def _():
            s_back, s_ahead = s_copies(k)
            pl.when(has_prev)(lambda: s_ahead.wait_recv())
            pl.when(has_next)(lambda: s_back.wait_recv())

        for w in range(2):
            sxx = [rx_s[k, 0, w], st[w, 3, 0], st[w, 3, 1], rx_s[k, 1, w]]
            for i in range(3):
                sxy = edge[w, 1] if i == 0 else st[w, 6, i - 1]
                sxz = edge[w, 2] if i == 0 else st[w, 7, i - 1]
                factor = edge_par[1] if i == 0 else par[2, i - 1]
                change = factor * ((sxx[i + 1] - sxx[i]) + (sxy - yp(sxy)) + (sxz - zp(sxz)))
                if i == 0:
                    edge[w, 0] = edge[w, 0] - change
                else:
                    st[w, 0, i - 1] = st[w, 0, i - 1] - change

        pl.when(k == steps - 1)(lambda: go_home(0))

        for i in range(2):
            terms = []
            at = pl.ds(i * ny, ny)
            gains = (amp[k, 0:1] * spot[at], DT * push[k, at])
            for w in range(2):
                vx0 = edge[w, 0] if i == 0 else st[w, 0, 0]
                vy, vz = st[w, 1, i], st[w, 2, i]
                exx = st[w, 0, i] - vx0
                eyy = vy - yp(vy)
                ezz = vz - zp(vz)
                tr = exx + eyy + ezz
                common = par[0, i] * tr + gains[w]
                twice = 2.0 * par[1, i]
                sxx = st[w, 3, i] - (common + twice * exx)
                st[w, 3, i] = sxx
                tx_s[k, i, w] = sxx
                st[w, 4, i] = st[w, 4, i] - (common + twice * eyy)
                st[w, 5, i] = st[w, 5, i] - (common + twice * ezz)
                terms.append((exx, eyy, ezz, tr))
            f, a = terms
            grad[0, i] += f[3] * a[3]
            grad[1, i] += 2.0 * (f[0] * a[0] + f[1] * a[1] + f[2] * a[2])

        @pl.when(k < steps - 1)
        def _():
            s_back = remote(
                tx_s.at[k, 0], rx_s.at[k + 1, 1], s_send.at[k, 0], s_recv.at[k + 1, 1], prev_dev
            )
            s_ahead = remote(
                tx_s.at[k, 1], rx_s.at[k + 1, 0], s_send.at[k, 1], s_recv.at[k + 1, 0], next_dev
            )
            pl.when(has_prev)(lambda: s_back.start())
            pl.when(has_next)(lambda: s_ahead.start())

        pl.when(k == steps - 1)(lambda: go_home(1))

        for i in range(2):
            eyz = []
            for w in range(2):
                vy, vz = st[w, 1, i], st[w, 2, i]
                strain = (zn(vy) - vy) + (yn(vz) - vz)
                st[w, 8, i] = st[w, 8, i] - par[1, i] * strain
                eyz.append(strain)
            grad[1, i] += eyz[0] * eyz[1]

        pl.when(k == steps - 1)(lambda: go_home(2))

        pl.when(has_prev)(lambda: ahead.wait_recv())
        pl.when(has_next)(lambda: back.wait_recv())
        for i in range(3):
            pair = []
            for w in range(2):
                vx = edge[w, 0] if i == 0 else st[w, 0, i - 1]
                vy0 = rx_v[k, 0, w, 0] if i == 0 else st[w, 1, i - 1]
                vz0 = rx_v[k, 0, w, 1] if i == 0 else st[w, 2, i - 1]
                vy1 = rx_v[k, 1, w, 0] if i == 2 else st[w, 1, i]
                vz1 = rx_v[k, 1, w, 1] if i == 2 else st[w, 2, i]
                exy = (yn(vx) - vx) + (vy1 - vy0)
                exz = (zn(vx) - vx) + (vz1 - vz0)
                if i == 0:
                    edge[w, 1] = edge[w, 1] - edge_par[0] * exy
                    edge[w, 2] = edge[w, 2] - edge_par[0] * exz
                else:
                    st[w, 6, i - 1] = st[w, 6, i - 1] - par[1, i - 1] * exy
                    st[w, 7, i - 1] = st[w, 7, i - 1] - par[1, i - 1] * exz
                pair.append((exy, exz))
            if i > 0:
                grad[1, i - 1] += pair[0][0] * pair[1][0] + pair[0][1] * pair[1][1]
        return carry

    lax.fori_loop(0, steps, step, 0)

    go_home(3)
    grad[...] = DT * grad[...]
    part = ny // n_shot

    def grad_remote(t):
        return remote(
            grad.at[:, :, pl.ds(t * part, part)],
            rx_grad.at[my_shot],
            grad_send.at[t],
            grad_recv.at[my_shot],
            (jnp.int32(t), my_slab),
        )

    for t in range(n_shot):
        own = jnp.logical_and(stays, t == shot)

        @pl.when(jnp.logical_not(own))
        def _(t=t):
            grad_remote(t).start()

        @pl.when(own)
        def _(t=t):
            rx_grad[t] = grad[:, :, t * part : (t + 1) * part]

    for t in range(n_shot):
        own = jnp.logical_and(stays, t == shot)

        @pl.when(jnp.logical_not(own))
        def _(t=t):
            remote(
                grad.at[:, :, pl.ds(t * part, part)],
                rx_grad.at[t],
                grad_send.at[t],
                grad_recv.at[t],
                (jnp.int32(t), my_slab),
            ).wait_recv()

    @pl.when(moves)
    def _():
        for n in range(len(groups)):
            home_away(n).wait_recv()
            home_land(n).start()

    total = rx_grad[0]
    for t in range(1, n_shot):
        total = total + rx_grad[t]
    lam_out[...] = total[0]
    mu_out[...] = total[1]

    for t in range(n_shot):
        own = jnp.logical_and(stays, t == shot)
        pl.when(jnp.logical_not(own))(lambda t=t: grad_remote(t).wait_send())

    def drain(k, carry):
        back, ahead = v_copies(k)
        pl.when(has_prev)(lambda: back.wait_send())
        pl.when(has_next)(lambda: ahead.wait_send())

        @pl.when(k < steps - 1)
        def _():
            s_back, s_ahead = s_copies(k)
            pl.when(has_prev)(lambda: s_back.wait_send())
            pl.when(has_next)(lambda: s_ahead.wait_send())

        return carry

    lax.fori_loop(0, steps, drain, 0)

    def drain_msg(t, carry):
        pl.when(jnp.logical_not(is_self(t)))(lambda: msg_copy(t).wait_send())
        return carry

    lax.fori_loop(0, n_slab, drain_msg, 0)

    @pl.when(sends_next)
    def _():
        for copy in next_copies:
            copy.wait_send()

    @pl.when(sends_prev)
    def _():
        for copy in prev_copies:
            copy.wait_send()

    @pl.when(stays)
    def _():
        for n in range(len(groups)):
            home_local(n).wait()

    @pl.when(moves)
    def _():
        for copy in swap_in:
            copy.wait_send()
        for n in range(len(groups)):
            home_away(n).wait_send()
            home_land(n).wait()


def deliver(a, b, c, a_out, b_out, c_out, a_mid, b_mid, c_mid, sem):
    pairs = ((a, a_mid, a_out), (b, b_mid, b_out), (c, c_mid, c_out))
    loads = [pltpu.make_async_copy(src, mid, sem.at[0, i]) for i, (src, mid, _) in enumerate(pairs)]
    stores = [pltpu.make_async_copy(mid, dst, sem.at[1, i]) for i, (_, mid, dst) in enumerate(pairs)]
    for copy in loads:
        copy.start()
    for load, store in zip(loads, stores):
        load.wait()
        store.start()
    for copy in stores:
        copy.wait()


def shards(n_shot, n_slab, lam, mu, buo, fwd, adj, wavelet, source, traces, rslab, rcell):
    planes, ny, nz = lam.shape
    steps = wavelet.shape[1]
    nrec = traces.shape[2]
    f32 = jnp.float32
    vmem = pl.BlockSpec(memory_space=pltpu.VMEM)
    hbm = pl.BlockSpec(memory_space=pl.ANY)
    dma = pltpu.SemaphoreType.DMA
    part = ny // n_shot
    outs = pl.pallas_call(
        functools.partial(kernel, n_shot, n_slab, steps),
        out_shape=(
            jax.ShapeDtypeStruct((1, 9, planes, ny, nz), f32),
            jax.ShapeDtypeStruct((planes, part, nz), f32),
            jax.ShapeDtypeStruct((planes, part, nz), f32),
        ),
        in_specs=[hbm] * 10,
        out_specs=(hbm, vmem, vmem),
        scratch_shapes=[
            pltpu.VMEM((1, steps), f32),
            pltpu.SMEM((1,), jnp.int32),
            pltpu.VMEM((1, steps, nrec), f32),
            pltpu.VMEM((1, nrec), jnp.int32),
            pltpu.VMEM((1, nrec), jnp.int32),
            dma((5,)),
            pltpu.VMEM((2, 9, planes, ny, nz), f32),
            pltpu.VMEM((3, planes, ny, nz), f32),
            pltpu.VMEM((2, 3, ny, nz), f32),
            pltpu.VMEM((2, ny, nz), f32),
            pltpu.VMEM((steps, 2, 2, ny, nz), f32),
            pltpu.VMEM((steps, 2, 2, 2, ny, nz), f32),
            pltpu.VMEM((steps, 2, 2, ny, nz), f32),
            pltpu.VMEM((steps, 2, 2, 2, ny, nz), f32),
            pltpu.VMEM((MSG, nrec), f32),
            pltpu.VMEM((n_slab, MSG, nrec), f32),
            pltpu.VMEM((steps, planes * ny, nz), f32),
            pltpu.VMEM((planes * ny, nz), f32),
            pltpu.VMEM((steps, 8, nz), f32),
            pltpu.VMEM((2, planes, ny, nz), f32),
            pltpu.VMEM((n_shot, 2, planes, part, nz), f32),
            pltpu.VMEM((2, 9, planes, ny, nz), f32),
            pltpu.VMEM((3, planes, ny, nz), f32),
            pltpu.VMEM((9, planes, ny, nz), f32),
            dma((5,)),
            dma((7,)),
            dma((4,)),
            dma((7,)),
            dma((5,)),
            dma((10,)),
            dma((10,)),
            dma((steps, 2)),
            dma((steps, 2)),
            dma((steps, 2)),
            dma((steps, 2)),
            dma((n_slab,)),
            dma((n_slab,)),
            dma((n_shot,)),
            dma((n_shot,)),
            dma((4,)),
            dma((4,)),
        ],
        compiler_params=pltpu.CompilerParams(
            has_side_effects=True, collective_id=0, vmem_limit_bytes=60 * 1024 * 1024
        ),
        cost_estimate=pl.CostEstimate(flops=10**7, bytes_accessed=10**6, transcendentals=0),
    )(
        lam,
        mu,
        buo,
        fwd,
        adj,
        wavelet,
        source,
        traces,
        rslab.reshape(1, nrec),
        rcell.reshape(1, nrec),
    )
    return pl.pallas_call(
        deliver,
        out_shape=tuple(jax.ShapeDtypeStruct(o.shape, o.dtype) for o in outs),
        in_specs=[hbm] * 3,
        out_specs=(hbm,) * 3,
        scratch_shapes=[pltpu.VMEM(o.shape, o.dtype) for o in outs] + [dma((2, 3))],
        compiler_params=pltpu.CompilerParams(vmem_limit_bytes=60 * 1024 * 1024),
        cost_estimate=pl.CostEstimate(flops=0, bytes_accessed=10**6, transcendentals=0),
    )(*outs)


def solution(mesh):
    in_specs = (
        P("slab", None, None),
        P("slab", None, None),
        P("slab", None, None),
        P("shot", None, "slab", None, None),
        P("shot", None, "slab", None, None),
        P("shot", None),
        P("shot"),
        P("shot", None, "slab"),
        P("slab", None),
        P("slab"),
    )
    out_specs = (
        P("shot", None, "slab", None, None),
        P("slab", "shot", None),
        P("slab", "shot", None),
    )
    body = functools.partial(shards, mesh.shape["shot"], mesh.shape["slab"])
    return jax.shard_map(body, mesh=mesh, in_specs=in_specs, out_specs=out_specs, check_vma=False)
```

```python
import functools
import jax
import jax.numpy as jnp
from jax import lax
from jax.experimental import pallas as pl
from jax.experimental.pallas import tpu as pltpu
from jax.sharding import PartitionSpec as P

DT = 0.3
MESH = pl.DeviceIdType.MESH
MSG = 16


def at_virtual(shot, slab):
    core, half = lax.rem(shot, 2), lax.rem(slab, 2)
    return (shot - core + half, slab - half + core)


def kernel(
    n_shot,
    n_slab,
    steps,
    lam_hbm,
    mu_hbm,
    buo_hbm,
    fwd_hbm,
    adj_hbm,
    wavelet_hbm,
    source_hbm,
    traces_hbm,
    rslab_hbm,
    rcell_hbm,
    adj_out,
    lam_out,
    mu_out,
    wavelet_ref,
    source_ref,
    traces_ref,
    rslab_ref,
    rcell_ref,
    small_sem,
    st,
    par,
    edge,
    edge_par,
    rx_s,
    rx_v,
    tx_s,
    tx_v,
    msg,
    rx_msg,
    push,
    spot,
    amp,
    grad,
    rx_grad,
    own,
    own_par,
    home,
    own_sem,
    swap_recv,
    home_sem,
    in_send,
    in_recv,
    edge_send,
    edge_recv,
    s_send,
    s_recv,
    v_send,
    v_recv,
    msg_send,
    msg_recv,
    grad_send,
    grad_recv,
    out_send,
    out_recv,
):
    ny, nz = st.shape[3], st.shape[4]
    cells = 2 * ny * nz
    rows = 2 * ny
    shot, slab = lax.axis_index("shot"), lax.axis_index("slab")
    my_shot, my_slab = at_virtual(shot, slab)
    stays = lax.rem(shot, 2) == lax.rem(slab, 2)
    moves = jnp.logical_not(stays)
    partner = (my_shot, my_slab)
    prev_dev = at_virtual(my_shot, jnp.maximum(my_slab - 1, 0))
    next_dev = at_virtual(my_shot, jnp.minimum(my_slab + 1, n_slab - 1))
    has_prev, has_next = my_slab > 0, my_slab < n_slab - 1

    def remote(src, dst, ssem, rsem, dev):
        return pltpu.make_async_remote_copy(
            src_ref=src, dst_ref=dst, send_sem=ssem, recv_sem=rsem, device_id=dev, device_id_type=MESH
        )

    small = [
        pltpu.make_async_copy(a, b, small_sem.at[i])
        for i, (a, b) in enumerate(
            (
                (wavelet_hbm, wavelet_ref),
                (source_hbm, source_ref),
                (traces_hbm, traces_ref),
                (rslab_hbm, rslab_ref),
                (rcell_hbm, rcell_ref),
            )
        )
    ]
    for copy in small:
        copy.start()
    own_pairs = [
        (fwd_hbm.at[0], own.at[0]),
        (adj_hbm.at[0], own.at[1]),
        (lam_hbm, own_par.at[0]),
        (mu_hbm, own_par.at[1]),
        (buo_hbm, own_par.at[2]),
    ]
    own_in = [pltpu.make_async_copy(a, b, own_sem.at[i]) for i, (a, b) in enumerate(own_pairs)]
    for copy in own_in:
        copy.start()
    work_pairs = [
        (fwd_hbm.at[0], st.at[0]),
        (adj_hbm.at[0], st.at[1]),
        (lam_hbm, par.at[0]),
        (mu_hbm, par.at[1]),
        (buo_hbm, par.at[2]),
    ]
    local_in = [pltpu.make_async_copy(a, b, in_recv.at[i]) for i, (a, b) in enumerate(work_pairs)]

    @pl.when(stays)
    def _():
        for copy in local_in:
            copy.start()

    first_shot, first_slab = shot - lax.rem(shot, 2), slab - lax.rem(slab, 2)
    barrier = pltpu.get_barrier_semaphore()

    def greet(q, carry):
        for core in range(2):
            me = jnp.logical_and(q == slab, first_shot + core == shot)

            @pl.when(jnp.logical_not(me))
            def _(core=core):
                pl.semaphore_signal(
                    barrier, inc=1, device_id=(first_shot + core, q), device_id_type=MESH
                )

        return carry

    lax.fori_loop(0, n_slab, greet, 0)
    for other in range(0, n_shot, 2):

        @pl.when(first_shot != other)
        def _(other=other):
            for t in (other, other + 1):
                for half in range(2):
                    pl.semaphore_signal(
                        barrier,
                        inc=1,
                        device_id=(jnp.int32(t), first_slab + half),
                        device_id_type=MESH,
                    )

    msg[...] = jnp.zeros_like(msg)
    for copy in small:
        copy.wait()
    msg[0:steps] = traces_ref[0]
    msg[steps : steps + 1] = rslab_ref[...].astype(jnp.float32)
    msg[steps + 1 : steps + 2] = rcell_ref[...].astype(jnp.float32)
    msg[steps + 2 : steps + 3, 0:steps] = wavelet_ref[...]
    msg[steps + 3 : steps + 4] = jnp.full((1, msg.shape[1]), source_ref[0], jnp.int32).astype(
        jnp.float32
    )

    pl.semaphore_wait(barrier, 2 * n_slab - 1 + 2 * (n_shot - 2))

    def msg_copy(t):
        return remote(msg, rx_msg.at[slab], msg_send.at[t], msg_recv.at[slab], at_virtual(shot, t))

    def msg_local():
        return pltpu.make_async_copy(msg, rx_msg.at[slab], msg_recv.at[slab])

    def is_self(t):
        return jnp.logical_and(stays, t == slab)

    def send_msg(t, carry):
        pl.when(jnp.logical_not(is_self(t)))(lambda: msg_copy(t).start())
        return carry

    lax.fori_loop(0, n_slab, send_msg, 0)
    pl.when(stays)(lambda: msg_local().start())

    orig_prev = at_virtual(shot, jnp.maximum(slab - 1, 0))
    orig_next = at_virtual(shot, jnp.minimum(slab + 1, n_slab - 1))
    sends_next, sends_prev = slab < n_slab - 1, slab > 0
    mat_next = [(own_par.at[1, 1], edge_par.at[0]), (own_par.at[2, 1], edge_par.at[1])]
    wave_next = [
        [
            (own.at[w, 6:8, 1], edge.at[w, 1:3]),
            (own.at[w, 0, 1], edge.at[w, 0]),
            (own.at[w, 3, 1], rx_s.at[0, 0, w]),
        ]
        for w in range(2)
    ]
    wave_prev = [[(own.at[w, 3, 0], rx_s.at[0, 1, w])] for w in range(2)]
    swaps = [[(own.at[w, a : a + 3], st.at[w, a : a + 3]) for a in (6, 3, 0)] for w in range(2)]

    def batch(pairs, ssem, rsem, start, dev):
        return [
            remote(a, b, ssem.at[start + n], rsem.at[start + n], dev) for n, (a, b) in enumerate(pairs)
        ]

    mat_edge = batch(mat_next, edge_send, edge_recv, 0, orig_next)
    mat_swap = batch([(own_par, par)], in_send, swap_recv, 0, partner)
    edge_next = [batch(wave_next[w], edge_send, edge_recv, 2 + 4 * w, orig_next) for w in range(2)]
    edge_prev = [batch(wave_prev[w], edge_send, edge_recv, 5 + 4 * w, orig_prev) for w in range(2)]
    wave_swap = [batch(swaps[w], in_send, swap_recv, 1 + 3 * w, partner) for w in range(2)]

    def when_all(condition, copies, action):
        @pl.when(condition)
        def _():
            for copy in copies:
                getattr(copy, action)()

    for copy in own_in[2:]:
        copy.wait()
    when_all(sends_next, mat_edge, "start")
    when_all(moves, mat_swap, "start")
    for w in range(2):
        own_in[w].wait()
        when_all(sends_next, edge_next[w], "start")
        when_all(sends_prev, edge_prev[w], "start")
        when_all(moves, wave_swap[w], "start")

    @pl.when(jnp.logical_not(has_prev))
    def _():
        edge[...] = jnp.zeros_like(edge)
        edge_par[...] = jnp.zeros_like(edge_par)
        rx_s[:, 0] = jnp.zeros((steps, 2, ny, nz), jnp.float32)
        rx_v[:, 0] = jnp.zeros((steps, 2, 2, ny, nz), jnp.float32)

    @pl.when(jnp.logical_not(has_next))
    def _():
        rx_s[:, 1] = jnp.zeros((steps, 2, ny, nz), jnp.float32)
        rx_v[:, 1] = jnp.zeros((steps, 2, 2, ny, nz), jnp.float32)

    grad[...] = jnp.zeros_like(grad)
    push[...] = jnp.zeros_like(push)

    nrec = msg.shape[1]
    row_of = lax.broadcasted_iota(jnp.int32, (rows, nrec), 0)
    col_of = lax.broadcasted_iota(jnp.int32, (nz, nrec), 0)

    def scatter(pair, carry):
        left, right = [], []
        for q in (2 * pair, 2 * pair + 1):
            pltpu.make_async_copy(msg, rx_msg.at[q], msg_recv.at[q]).wait()
            block = rx_msg[q]
            named = block[steps : steps + 1].astype(jnp.int32)
            cell = block[steps + 1 : steps + 2].astype(jnp.int32)
            row = jnp.where(named == my_slab, cell // nz, -1)
            hit = row_of == row
            column = (col_of == lax.rem(cell, nz)).astype(jnp.float32).astype(jnp.bfloat16)
            trace = block[0:steps]
            high = trace.astype(jnp.bfloat16).astype(jnp.float32)
            low = trace - high
            left.append(
                jnp.concatenate(
                    [
                        jnp.where(hit, term[k : k + 1], 0.0).astype(jnp.bfloat16)
                        for term in (high, low)
                        for k in range(steps)
                    ],
                    axis=0,
                )
            )
            right.append(column)
        out = lax.dot_general(
            jnp.concatenate(left, axis=1),
            jnp.concatenate(right, axis=1),
            (((1,), (1,)), ((), ())),
            preferred_element_type=jnp.float32,
        )
        for k in range(steps):
            push[k] += out[k * rows : (k + 1) * rows] + out[(steps + k) * rows : (steps + k + 1) * rows]
        return carry

    lax.fori_loop(0, n_slab // 2, scatter, 0)

    head = rx_msg[my_slab]
    source = head[steps + 3 : steps + 4].astype(jnp.int32) - my_slab * cells
    flat = lax.broadcasted_iota(jnp.int32, (rows, nz), 0) * nz
    flat = flat + lax.broadcasted_iota(jnp.int32, (rows, nz), 1)
    spot[...] = (flat == source).astype(jnp.float32)
    for k in range(steps):
        amp[k] = jnp.broadcast_to(DT * head[steps + 2 : steps + 3, k : k + 1], (8, nz))

    when_all(stays, local_in[2:], "wait")
    when_all(moves, mat_swap, "wait_recv")
    when_all(has_prev, mat_edge, "wait_recv")

    y_at = lax.broadcasted_iota(jnp.int32, (ny, nz), 0)
    z_at = lax.broadcasted_iota(jnp.int32, (ny, nz), 1)

    def yn(a):
        return jnp.where(y_at < ny - 1, pltpu.roll(a, ny - 1, 0), 0.0)

    def yp(a):
        return jnp.where(y_at > 0, pltpu.roll(a, 1, 0), 0.0)

    def zn(a):
        return jnp.where(z_at < nz - 1, pltpu.roll(a, nz - 1, 1), 0.0)

    def zp(a):
        return jnp.where(z_at > 0, pltpu.roll(a, 1, 1), 0.0)

    par[0] = DT * par[0]
    par[1] = DT * par[1]
    par[2] = DT * par[2]
    edge_par[...] = DT * edge_par[...]

    def v_back(k, w):
        return remote(
            tx_v.at[k, 0, w], rx_v.at[k, 1, w], v_send.at[k, 0, w], v_recv.at[k, 1, w], prev_dev
        )

    def v_ahead(k, w):
        return remote(
            tx_v.at[k, 1, w], rx_v.at[k, 0, w], v_send.at[k, 1, w], v_recv.at[k, 0, w], next_dev
        )

    def s_back(k, w):
        return remote(
            tx_s.at[k, 0, w], rx_s.at[k, 1, w], s_send.at[k, 0, w], s_recv.at[k, 1, w], prev_dev
        )

    def s_ahead(k, w):
        return remote(
            tx_s.at[k, 1, w], rx_s.at[k, 0, w], s_send.at[k, 1, w], s_recv.at[k, 0, w], next_dev
        )

    groups = ((0, 3), (3, 6), (8, 9), (6, 8))

    def home_local(n):
        a, b = groups[n]
        return pltpu.make_async_copy(st.at[1, a:b], adj_out.at[0, a:b], home_sem.at[n])

    def home_land(n):
        a, b = groups[n]
        return pltpu.make_async_copy(home.at[a:b], adj_out.at[0, a:b], home_sem.at[n])

    def home_away(n):
        a, b = groups[n]
        return remote(st.at[1, a:b], home.at[a:b], out_send.at[n], out_recv.at[n], partner)

    def go_home(n):
        pl.when(stays)(lambda: home_local(n).start())
        pl.when(moves)(lambda: home_away(n).start())

    def transverse(k, w):
        for i in range(2):
            sxy0 = edge[w, 1] if i == 0 else st[w, 6, 0]
            sxz0 = edge[w, 2] if i == 0 else st[w, 7, 0]
            syy, szz, syz = st[w, 4, i], st[w, 5, i], st[w, 8, i]
            vy = st[w, 1, i] - par[2, i] * (
                (st[w, 6, i] - sxy0) + (yn(syy) - syy) + (syz - zp(syz))
            )
            vz = st[w, 2, i] - par[2, i] * (
                (st[w, 7, i] - sxz0) + (syz - yp(syz)) + (zn(szz) - szz)
            )
            st[w, 1, i] = vy
            st[w, 2, i] = vz
            tx_v[k, i, w, 0] = vy
            tx_v[k, i, w, 1] = vz
        pl.when(has_prev)(lambda: v_back(k, w).start())
        pl.when(has_next)(lambda: v_ahead(k, w).start())

    def step(k, carry):
        normal = []
        for w in range(2):
            @pl.when(k > 0)
            def _(w=w):
                pl.when(has_prev)(lambda: s_ahead(k, w).wait_recv())
                pl.when(has_next)(lambda: s_back(k, w).wait_recv())

            sxx = [rx_s[k, 0, w], st[w, 3, 0], st[w, 3, 1], rx_s[k, 1, w]]
            for i in range(3):
                sxy = edge[w, 1] if i == 0 else st[w, 6, i - 1]
                sxz = edge[w, 2] if i == 0 else st[w, 7, i - 1]
                factor = edge_par[1] if i == 0 else par[2, i - 1]
                change = factor * ((sxx[i + 1] - sxx[i]) + (sxy - yp(sxy)) + (sxz - zp(sxz)))
                if i == 0:
                    edge[w, 0] = edge[w, 0] - change
                else:
                    st[w, 0, i - 1] = st[w, 0, i - 1] - change

            terms = []
            for i in range(2):
                at = pl.ds(i * ny, ny)
                gain = amp[k, 0:1] * spot[at] if w == 0 else DT * push[k, at]
                vx0 = edge[w, 0] if i == 0 else st[w, 0, 0]
                vy, vz = st[w, 1, i], st[w, 2, i]
                exx = st[w, 0, i] - vx0
                eyy = vy - yp(vy)
                ezz = vz - zp(vz)
                tr = exx + eyy + ezz
                common = par[0, i] * tr + gain
                twice = 2.0 * par[1, i]
                new = st[w, 3, i] - (common + twice * exx)
                st[w, 3, i] = new
                tx_s[k, i, w] = new
                st[w, 4, i] = st[w, 4, i] - (common + twice * eyy)
                st[w, 5, i] = st[w, 5, i] - (common + twice * ezz)
                terms.append((exx, eyy, ezz, tr))
            normal.append(terms)

            @pl.when(k < steps - 1)
            def _(w=w):
                back = remote(
                    tx_s.at[k, 0, w],
                    rx_s.at[k + 1, 1, w],
                    s_send.at[k, 0, w],
                    s_recv.at[k + 1, 1, w],
                    prev_dev,
                )
                ahead = remote(
                    tx_s.at[k, 1, w],
                    rx_s.at[k + 1, 0, w],
                    s_send.at[k, 1, w],
                    s_recv.at[k + 1, 0, w],
                    next_dev,
                )
                pl.when(has_prev)(lambda: back.start())
                pl.when(has_next)(lambda: ahead.start())

        @pl.when(k == steps - 1)
        def _():
            go_home(0)
            go_home(1)

        for i in range(2):
            f, a = normal[0][i], normal[1][i]
            grad[0, i] += f[3] * a[3]
            eyz = []
            for w in range(2):
                vy, vz = st[w, 1, i], st[w, 2, i]
                strain = (zn(vy) - vy) + (yn(vz) - vz)
                st[w, 8, i] = st[w, 8, i] - par[1, i] * strain
                eyz.append(strain)
            grad[1, i] += 2.0 * (f[0] * a[0] + f[1] * a[1] + f[2] * a[2]) + eyz[0] * eyz[1]

        pl.when(k == steps - 1)(lambda: go_home(2))

        shear = []
        for w in range(2):
            pl.when(has_prev)(lambda: v_ahead(k, w).wait_recv())
            pl.when(has_next)(lambda: v_back(k, w).wait_recv())
            strains = []
            for i in range(3):
                vx = edge[w, 0] if i == 0 else st[w, 0, i - 1]
                vy0 = rx_v[k, 0, w, 0] if i == 0 else st[w, 1, i - 1]
                vz0 = rx_v[k, 0, w, 1] if i == 0 else st[w, 2, i - 1]
                vy1 = rx_v[k, 1, w, 0] if i == 2 else st[w, 1, i]
                vz1 = rx_v[k, 1, w, 1] if i == 2 else st[w, 2, i]
                exy = (yn(vx) - vx) + (vy1 - vy0)
                exz = (zn(vx) - vx) + (vz1 - vz0)
                if i == 0:
                    edge[w, 1] = edge[w, 1] - edge_par[0] * exy
                    edge[w, 2] = edge[w, 2] - edge_par[0] * exz
                else:
                    st[w, 6, i - 1] = st[w, 6, i - 1] - par[1, i - 1] * exy
                    st[w, 7, i - 1] = st[w, 7, i - 1] - par[1, i - 1] * exz
                    strains.append((exy, exz))
            shear.append(strains)
            pl.when(k < steps - 1)(lambda w=w: transverse(k + 1, w))

        for i in range(2):
            f, a = shear[0][i], shear[1][i]
            grad[1, i] += f[0] * a[0] + f[1] * a[1]
        return carry

    for w in range(2):
        when_all(stays, local_in[w : w + 1], "wait")
        when_all(moves, wave_swap[w], "wait_recv")
        when_all(has_prev, edge_next[w], "wait_recv")
        when_all(has_next, edge_prev[w], "wait_recv")
        transverse(0, w)
    lax.fori_loop(0, steps, step, 0)

    go_home(3)
    grad[...] = DT * grad[...]
    part = ny // n_shot

    def grad_remote(t):
        return remote(
            grad.at[:, :, pl.ds(t * part, part)],
            rx_grad.at[my_shot],
            grad_send.at[t],
            grad_recv.at[my_shot],
            (jnp.int32(t), my_slab),
        )

    for t in range(n_shot):
        own = jnp.logical_and(stays, t == shot)

        @pl.when(jnp.logical_not(own))
        def _(t=t):
            grad_remote(t).start()

        @pl.when(own)
        def _(t=t):
            rx_grad[t] = grad[:, :, t * part : (t + 1) * part]

    for t in range(n_shot):
        own = jnp.logical_and(stays, t == shot)

        @pl.when(jnp.logical_not(own))
        def _(t=t):
            remote(
                grad.at[:, :, pl.ds(t * part, part)],
                rx_grad.at[t],
                grad_send.at[t],
                grad_recv.at[t],
                (jnp.int32(t), my_slab),
            ).wait_recv()

    @pl.when(moves)
    def _():
        for n in range(len(groups)):
            home_away(n).wait_recv()
            home_land(n).start()

    total = rx_grad[0]
    for t in range(1, n_shot):
        total = total + rx_grad[t]
    lam_out[...] = total[0]
    mu_out[...] = total[1]

    for t in range(n_shot):
        own = jnp.logical_and(stays, t == shot)
        pl.when(jnp.logical_not(own))(lambda t=t: grad_remote(t).wait_send())

    def drain(k, carry):
        for w in range(2):
            pl.when(has_prev)(lambda: v_back(k, w).wait_send())
            pl.when(has_next)(lambda: v_ahead(k, w).wait_send())

            @pl.when(k < steps - 1)
            def _(w=w):
                pl.when(has_prev)(lambda: s_back(k, w).wait_send())
                pl.when(has_next)(lambda: s_ahead(k, w).wait_send())

        return carry

    lax.fori_loop(0, steps, drain, 0)

    def drain_msg(t, carry):
        pl.when(jnp.logical_not(is_self(t)))(lambda: msg_copy(t).wait_send())
        return carry

    lax.fori_loop(0, n_slab, drain_msg, 0)

    when_all(sends_next, mat_edge + edge_next[0] + edge_next[1], "wait_send")
    when_all(sends_prev, edge_prev[0] + edge_prev[1], "wait_send")
    when_all(moves, mat_swap + wave_swap[0] + wave_swap[1], "wait_send")

    @pl.when(stays)
    def _():
        for n in range(len(groups)):
            home_local(n).wait()

    @pl.when(moves)
    def _():
        for n in range(len(groups)):
            home_away(n).wait_send()
            home_land(n).wait()


def deliver(a, b, c, a_out, b_out, c_out, a_mid, b_mid, c_mid, sem):
    pairs = ((a, a_mid, a_out), (b, b_mid, b_out), (c, c_mid, c_out))
    loads = [pltpu.make_async_copy(src, mid, sem.at[0, i]) for i, (src, mid, _) in enumerate(pairs)]
    stores = [pltpu.make_async_copy(mid, dst, sem.at[1, i]) for i, (_, mid, dst) in enumerate(pairs)]
    for copy in loads:
        copy.start()
    for load, store in zip(loads, stores):
        load.wait()
        store.start()
    for copy in stores:
        copy.wait()


def shards(n_shot, n_slab, lam, mu, buo, fwd, adj, wavelet, source, traces, rslab, rcell):
    planes, ny, nz = lam.shape
    steps = wavelet.shape[1]
    nrec = traces.shape[2]
    f32 = jnp.float32
    vmem = pl.BlockSpec(memory_space=pltpu.VMEM)
    hbm = pl.BlockSpec(memory_space=pl.ANY)
    dma = pltpu.SemaphoreType.DMA
    part = ny // n_shot
    outs = pl.pallas_call(
        functools.partial(kernel, n_shot, n_slab, steps),
        out_shape=(
            jax.ShapeDtypeStruct((1, 9, planes, ny, nz), f32),
            jax.ShapeDtypeStruct((planes, part, nz), f32),
            jax.ShapeDtypeStruct((planes, part, nz), f32),
        ),
        in_specs=[hbm] * 10,
        out_specs=(hbm, vmem, vmem),
        scratch_shapes=[
            pltpu.VMEM((1, steps), f32),
            pltpu.SMEM((1,), jnp.int32),
            pltpu.VMEM((1, steps, nrec), f32),
            pltpu.VMEM((1, nrec), jnp.int32),
            pltpu.VMEM((1, nrec), jnp.int32),
            dma((5,)),
            pltpu.VMEM((2, 9, planes, ny, nz), f32),
            pltpu.VMEM((3, planes, ny, nz), f32),
            pltpu.VMEM((2, 3, ny, nz), f32),
            pltpu.VMEM((2, ny, nz), f32),
            pltpu.VMEM((steps, 2, 2, ny, nz), f32),
            pltpu.VMEM((steps, 2, 2, 2, ny, nz), f32),
            pltpu.VMEM((steps, 2, 2, ny, nz), f32),
            pltpu.VMEM((steps, 2, 2, 2, ny, nz), f32),
            pltpu.VMEM((MSG, nrec), f32),
            pltpu.VMEM((n_slab, MSG, nrec), f32),
            pltpu.VMEM((steps, planes * ny, nz), f32),
            pltpu.VMEM((planes * ny, nz), f32),
            pltpu.VMEM((steps, 8, nz), f32),
            pltpu.VMEM((2, planes, ny, nz), f32),
            pltpu.VMEM((n_shot, 2, planes, part, nz), f32),
            pltpu.VMEM((2, 9, planes, ny, nz), f32),
            pltpu.VMEM((3, planes, ny, nz), f32),
            pltpu.VMEM((9, planes, ny, nz), f32),
            dma((5,)),
            dma((7,)),
            dma((4,)),
            dma((7,)),
            dma((5,)),
            dma((10,)),
            dma((10,)),
            dma((steps, 2, 2)),
            dma((steps, 2, 2)),
            dma((steps, 2, 2)),
            dma((steps, 2, 2)),
            dma((n_slab,)),
            dma((n_slab,)),
            dma((n_shot,)),
            dma((n_shot,)),
            dma((4,)),
            dma((4,)),
        ],
        compiler_params=pltpu.CompilerParams(
            has_side_effects=True, collective_id=0, vmem_limit_bytes=60 * 1024 * 1024
        ),
        cost_estimate=pl.CostEstimate(flops=10**7, bytes_accessed=10**6, transcendentals=0),
    )(
        lam,
        mu,
        buo,
        fwd,
        adj,
        wavelet,
        source,
        traces,
        rslab.reshape(1, nrec),
        rcell.reshape(1, nrec),
    )
    return pl.pallas_call(
        deliver,
        out_shape=tuple(jax.ShapeDtypeStruct(o.shape, o.dtype) for o in outs),
        in_specs=[hbm] * 3,
        out_specs=(hbm,) * 3,
        scratch_shapes=[pltpu.VMEM(o.shape, o.dtype) for o in outs] + [dma((2, 3))],
        compiler_params=pltpu.CompilerParams(vmem_limit_bytes=60 * 1024 * 1024),
        cost_estimate=pl.CostEstimate(flops=0, bytes_accessed=10**6, transcendentals=0),
    )(*outs)


def solution(mesh):
    in_specs = (
        P("slab", None, None),
        P("slab", None, None),
        P("slab", None, None),
        P("shot", None, "slab", None, None),
        P("shot", None, "slab", None, None),
        P("shot", None),
        P("shot"),
        P("shot", None, "slab"),
        P("slab", None),
        P("slab"),
    )
    out_specs = (
        P("shot", None, "slab", None, None),
        P("slab", "shot", None),
        P("slab", "shot", None),
    )
    body = functools.partial(shards, mesh.shape["shot"], mesh.shape["slab"])
    return jax.shard_map(body, mesh=mesh, in_specs=in_specs, out_specs=out_specs, check_vma=False)
```

```python
import functools
import jax
import jax.numpy as jnp
from jax import lax
from jax.experimental import pallas as pl
from jax.experimental.pallas import tpu as pltpu
from jax.sharding import PartitionSpec as P

DT = 0.3
MESH = pl.DeviceIdType.MESH
MSG = 16
LEAD = 2


def at_virtual(shot, slab):
    core, half = lax.rem(shot, 2), lax.rem(slab, 2)
    return (shot - core + half, slab - half + core)


def kernel(
    n_shot,
    n_slab,
    steps,
    lam_hbm,
    mu_hbm,
    buo_hbm,
    fwd_hbm,
    adj_hbm,
    wavelet_hbm,
    source_hbm,
    traces_hbm,
    rslab_hbm,
    rcell_hbm,
    adj_out,
    lam_out,
    mu_out,
    wavelet_ref,
    source_ref,
    traces_ref,
    rslab_ref,
    rcell_ref,
    small_sem,
    st,
    par,
    edge,
    edge_par,
    rx_s,
    rx_v,
    tx_s,
    tx_v,
    msg,
    rx_msg,
    push,
    spot,
    amp,
    grad,
    rx_grad,
    kept,
    own,
    own_par,
    home,
    own_sem,
    swap_recv,
    home_sem,
    in_send,
    in_recv,
    edge_send,
    edge_recv,
    s_send,
    s_recv,
    v_send,
    v_recv,
    msg_send,
    msg_recv,
    grad_send,
    grad_recv,
    out_send,
    out_recv,
):
    ny, nz = st.shape[3], st.shape[4]
    cells = 2 * ny * nz
    rows = 2 * ny
    shot, slab = lax.axis_index("shot"), lax.axis_index("slab")
    my_shot, my_slab = at_virtual(shot, slab)
    stays = lax.rem(shot, 2) == lax.rem(slab, 2)
    moves = jnp.logical_not(stays)
    partner = (my_shot, my_slab)
    prev_dev = at_virtual(my_shot, jnp.maximum(my_slab - 1, 0))
    next_dev = at_virtual(my_shot, jnp.minimum(my_slab + 1, n_slab - 1))
    has_prev, has_next = my_slab > 0, my_slab < n_slab - 1

    def remote(src, dst, ssem, rsem, dev):
        return pltpu.make_async_remote_copy(
            src_ref=src, dst_ref=dst, send_sem=ssem, recv_sem=rsem, device_id=dev, device_id_type=MESH
        )

    small = [
        pltpu.make_async_copy(a, b, small_sem.at[i])
        for i, (a, b) in enumerate(
            (
                (wavelet_hbm, wavelet_ref),
                (source_hbm, source_ref),
                (traces_hbm, traces_ref),
                (rslab_hbm, rslab_ref),
                (rcell_hbm, rcell_ref),
            )
        )
    ]
    for copy in small:
        copy.start()
    own_pairs = [
        (fwd_hbm.at[0], own.at[0]),
        (adj_hbm.at[0], own.at[1]),
        (lam_hbm, own_par.at[0]),
        (mu_hbm, own_par.at[1]),
        (buo_hbm, own_par.at[2]),
    ]
    own_in = [pltpu.make_async_copy(a, b, own_sem.at[i]) for i, (a, b) in enumerate(own_pairs)]
    for copy in own_in:
        copy.start()
    work_pairs = [
        (fwd_hbm.at[0], st.at[0]),
        (adj_hbm.at[0], st.at[1]),
        (lam_hbm, par.at[0]),
        (mu_hbm, par.at[1]),
        (buo_hbm, par.at[2]),
    ]
    local_in = [pltpu.make_async_copy(a, b, in_recv.at[i]) for i, (a, b) in enumerate(work_pairs)]

    @pl.when(stays)
    def _():
        for copy in local_in:
            copy.start()

    first_shot, first_slab = shot - lax.rem(shot, 2), slab - lax.rem(slab, 2)
    barrier = pltpu.get_barrier_semaphore()

    def greet(q, carry):
        for core in range(2):
            me = jnp.logical_and(q == slab, first_shot + core == shot)

            @pl.when(jnp.logical_not(me))
            def _(core=core):
                pl.semaphore_signal(
                    barrier, inc=1, device_id=(first_shot + core, q), device_id_type=MESH
                )

        return carry

    lax.fori_loop(0, n_slab, greet, 0)
    for other in range(0, n_shot, 2):

        @pl.when(first_shot != other)
        def _(other=other):
            for t in (other, other + 1):
                for half in range(2):
                    pl.semaphore_signal(
                        barrier,
                        inc=1,
                        device_id=(jnp.int32(t), first_slab + half),
                        device_id_type=MESH,
                    )

    msg[...] = jnp.zeros_like(msg)
    for copy in small:
        copy.wait()
    msg[0:steps] = traces_ref[0]
    msg[steps : steps + 1] = rslab_ref[...].astype(jnp.float32)
    msg[steps + 1 : steps + 2] = rcell_ref[...].astype(jnp.float32)
    msg[steps + 2 : steps + 3, 0:steps] = wavelet_ref[...]
    msg[steps + 3 : steps + 4] = jnp.full((1, msg.shape[1]), source_ref[0], jnp.int32).astype(
        jnp.float32
    )

    pl.semaphore_wait(barrier, 2 * n_slab - 1 + 2 * (n_shot - 2))

    def msg_copy(t):
        return remote(msg, rx_msg.at[slab], msg_send.at[t], msg_recv.at[slab], at_virtual(shot, t))

    def msg_local():
        return pltpu.make_async_copy(msg, rx_msg.at[slab], msg_recv.at[slab])

    def is_self(t):
        return jnp.logical_and(stays, t == slab)

    def send_msg(t, carry):
        pl.when(jnp.logical_not(is_self(t)))(lambda: msg_copy(t).start())
        return carry

    lax.fori_loop(0, n_slab, send_msg, 0)
    pl.when(stays)(lambda: msg_local().start())

    orig_prev = at_virtual(shot, jnp.maximum(slab - 1, 0))
    orig_next = at_virtual(shot, jnp.minimum(slab + 1, n_slab - 1))
    sends_next, sends_prev = slab < n_slab - 1, slab > 0
    mat_next = [(own_par.at[1, 1], edge_par.at[0]), (own_par.at[2, 1], edge_par.at[1])]
    wave_next = [
        [
            (own.at[w, 6:8, 1], edge.at[w, 1:3]),
            (own.at[w, 0, 1], edge.at[w, 0]),
            (own.at[w, 3, 1], rx_s.at[0, 0, w]),
        ]
        for w in range(2)
    ]
    wave_prev = [[(own.at[w, 3, 0], rx_s.at[0, 1, w])] for w in range(2)]
    swaps = [[(own.at[w, a : a + 3], st.at[w, a : a + 3]) for a in (6, 3, 0)] for w in range(2)]

    def batch(pairs, ssem, rsem, start, dev):
        return [
            remote(a, b, ssem.at[start + n], rsem.at[start + n], dev) for n, (a, b) in enumerate(pairs)
        ]

    mat_edge = batch(mat_next, edge_send, edge_recv, 0, orig_next)
    mat_swap = batch([(own_par, par)], in_send, swap_recv, 0, partner)
    edge_next = [batch(wave_next[w], edge_send, edge_recv, 2 + 4 * w, orig_next) for w in range(2)]
    edge_prev = [batch(wave_prev[w], edge_send, edge_recv, 5 + 4 * w, orig_prev) for w in range(2)]
    wave_swap = [batch(swaps[w], in_send, swap_recv, 1 + 3 * w, partner) for w in range(2)]

    def when_all(condition, copies, action):
        @pl.when(condition)
        def _():
            for copy in copies:
                getattr(copy, action)()

    for copy in own_in[2:]:
        copy.wait()
    when_all(sends_next, mat_edge, "start")
    when_all(moves, mat_swap, "start")
    for w in (1, 0):
        own_in[w].wait()
        when_all(sends_next, edge_next[w], "start")
        when_all(sends_prev, edge_prev[w], "start")
        when_all(moves, wave_swap[w], "start")

    @pl.when(jnp.logical_not(has_prev))
    def _():
        edge[...] = jnp.zeros_like(edge)
        edge_par[...] = jnp.zeros_like(edge_par)
        rx_s[:, 0] = jnp.zeros((steps, 2, ny, nz), jnp.float32)
        rx_v[:, 0] = jnp.zeros((steps, 2, 2, ny, nz), jnp.float32)

    @pl.when(jnp.logical_not(has_next))
    def _():
        rx_s[:, 1] = jnp.zeros((steps, 2, ny, nz), jnp.float32)
        rx_v[:, 1] = jnp.zeros((steps, 2, 2, ny, nz), jnp.float32)

    grad[...] = jnp.zeros_like(grad)
    push[...] = jnp.zeros_like(push)

    nrec = msg.shape[1]
    row_of = lax.broadcasted_iota(jnp.int32, (rows, nrec), 0)
    col_of = lax.broadcasted_iota(jnp.int32, (nz, nrec), 0)

    def scatter(pair, carry):
        left, right = [], []
        for q in (2 * pair, 2 * pair + 1):
            pltpu.make_async_copy(msg, rx_msg.at[q], msg_recv.at[q]).wait()
            block = rx_msg[q]
            named = block[steps : steps + 1].astype(jnp.int32)
            cell = block[steps + 1 : steps + 2].astype(jnp.int32)
            row = jnp.where(named == my_slab, cell // nz, -1)
            hit = row_of == row
            column = (col_of == lax.rem(cell, nz)).astype(jnp.float32).astype(jnp.bfloat16)
            trace = block[0:steps]
            high = trace.astype(jnp.bfloat16).astype(jnp.float32)
            low = trace - high
            left.append(
                jnp.concatenate(
                    [
                        jnp.where(hit, term[k : k + 1], 0.0).astype(jnp.bfloat16)
                        for term in (high, low)
                        for k in range(steps)
                    ],
                    axis=0,
                )
            )
            right.append(column)
        out = lax.dot_general(
            jnp.concatenate(left, axis=1),
            jnp.concatenate(right, axis=1),
            (((1,), (1,)), ((), ())),
            preferred_element_type=jnp.float32,
        )
        for k in range(steps):
            push[k] += out[k * rows : (k + 1) * rows] + out[(steps + k) * rows : (steps + k + 1) * rows]
        return carry

    lax.fori_loop(0, n_slab // 2, scatter, 0)

    head = rx_msg[my_slab]
    source = head[steps + 3 : steps + 4].astype(jnp.int32) - my_slab * cells
    flat = lax.broadcasted_iota(jnp.int32, (rows, nz), 0) * nz
    flat = flat + lax.broadcasted_iota(jnp.int32, (rows, nz), 1)
    spot[...] = (flat == source).astype(jnp.float32)
    for k in range(steps):
        amp[k] = jnp.broadcast_to(DT * head[steps + 2 : steps + 3, k : k + 1], (8, nz))

    when_all(stays, local_in[2:], "wait")
    when_all(moves, mat_swap, "wait_recv")
    when_all(has_prev, mat_edge, "wait_recv")

    y_at = lax.broadcasted_iota(jnp.int32, (ny, nz), 0)
    z_at = lax.broadcasted_iota(jnp.int32, (ny, nz), 1)

    def yn(a):
        return jnp.where(y_at < ny - 1, pltpu.roll(a, ny - 1, 0), 0.0)

    def yp(a):
        return jnp.where(y_at > 0, pltpu.roll(a, 1, 0), 0.0)

    def zn(a):
        return jnp.where(z_at < nz - 1, pltpu.roll(a, nz - 1, 1), 0.0)

    def zp(a):
        return jnp.where(z_at > 0, pltpu.roll(a, 1, 1), 0.0)

    par[0] = DT * par[0]
    par[1] = DT * par[1]
    par[2] = DT * par[2]
    edge_par[...] = DT * edge_par[...]

    def v_back(k, w):
        return remote(
            tx_v.at[k, 0, w], rx_v.at[k, 1, w], v_send.at[k, 0, w], v_recv.at[k, 1, w], prev_dev
        )

    def v_ahead(k, w):
        return remote(
            tx_v.at[k, 1, w], rx_v.at[k, 0, w], v_send.at[k, 1, w], v_recv.at[k, 0, w], next_dev
        )

    def s_back(k, w):
        return remote(
            tx_s.at[k, 0, w], rx_s.at[k, 1, w], s_send.at[k, 0, w], s_recv.at[k, 1, w], prev_dev
        )

    def s_ahead(k, w):
        return remote(
            tx_s.at[k, 1, w], rx_s.at[k, 0, w], s_send.at[k, 1, w], s_recv.at[k, 0, w], next_dev
        )

    groups = ((0, 3), (3, 6), (8, 9), (6, 8))

    def home_local(n):
        a, b = groups[n]
        return pltpu.make_async_copy(st.at[1, a:b], adj_out.at[0, a:b], home_sem.at[n])

    def home_land(n):
        a, b = groups[n]
        return pltpu.make_async_copy(home.at[a:b], adj_out.at[0, a:b], home_sem.at[n])

    def home_away(n):
        a, b = groups[n]
        return remote(st.at[1, a:b], home.at[a:b], out_send.at[n], out_recv.at[n], partner)

    def go_home(n):
        pl.when(stays)(lambda: home_local(n).start())
        pl.when(moves)(lambda: home_away(n).start())

    def transverse(k, w):
        for i in range(2):
            sxy0 = edge[w, 1] if i == 0 else st[w, 6, 0]
            sxz0 = edge[w, 2] if i == 0 else st[w, 7, 0]
            syy, szz, syz = st[w, 4, i], st[w, 5, i], st[w, 8, i]
            vy = st[w, 1, i] - par[2, i] * (
                (st[w, 6, i] - sxy0) + (yn(syy) - syy) + (syz - zp(syz))
            )
            vz = st[w, 2, i] - par[2, i] * (
                (st[w, 7, i] - sxz0) + (syz - yp(syz)) + (zn(szz) - szz)
            )
            st[w, 1, i] = vy
            st[w, 2, i] = vz
            tx_v[k, i, w, 0] = vy
            tx_v[k, i, w, 1] = vz
        pl.when(has_prev)(lambda: v_back(k, w).start())
        pl.when(has_next)(lambda: v_ahead(k, w).start())

    def normal(k, w):
        @pl.when(k > 0)
        def _():
            pl.when(has_prev)(lambda: s_ahead(k, w).wait_recv())
            pl.when(has_next)(lambda: s_back(k, w).wait_recv())

        sxx = [rx_s[k, 0, w], st[w, 3, 0], st[w, 3, 1], rx_s[k, 1, w]]
        for i in range(3):
            sxy = edge[w, 1] if i == 0 else st[w, 6, i - 1]
            sxz = edge[w, 2] if i == 0 else st[w, 7, i - 1]
            factor = edge_par[1] if i == 0 else par[2, i - 1]
            change = factor * ((sxx[i + 1] - sxx[i]) + (sxy - yp(sxy)) + (sxz - zp(sxz)))
            if i == 0:
                edge[w, 0] = edge[w, 0] - change
            else:
                st[w, 0, i - 1] = st[w, 0, i - 1] - change

        terms = []
        for i in range(2):
            at = pl.ds(i * ny, ny)
            gain = amp[k, 0:1] * spot[at] if w == 0 else DT * push[k, at]
            vx0 = edge[w, 0] if i == 0 else st[w, 0, 0]
            vy, vz = st[w, 1, i], st[w, 2, i]
            exx = st[w, 0, i] - vx0
            eyy = vy - yp(vy)
            ezz = vz - zp(vz)
            tr = exx + eyy + ezz
            common = par[0, i] * tr + gain
            twice = 2.0 * par[1, i]
            new = st[w, 3, i] - (common + twice * exx)
            st[w, 3, i] = new
            tx_s[k, i, w] = new
            st[w, 4, i] = st[w, 4, i] - (common + twice * eyy)
            st[w, 5, i] = st[w, 5, i] - (common + twice * ezz)
            terms.append((exx, eyy, ezz, tr))

        @pl.when(k < steps - 1)
        def _():
            back = remote(
                tx_s.at[k, 0, w],
                rx_s.at[k + 1, 1, w],
                s_send.at[k, 0, w],
                s_recv.at[k + 1, 1, w],
                prev_dev,
            )
            ahead = remote(
                tx_s.at[k, 1, w],
                rx_s.at[k + 1, 0, w],
                s_send.at[k, 1, w],
                s_recv.at[k + 1, 0, w],
                next_dev,
            )
            pl.when(has_prev)(lambda: back.start())
            pl.when(has_next)(lambda: ahead.start())

        if w == 1:

            @pl.when(k == steps - 1)
            def _():
                go_home(0)
                go_home(1)

        for i in range(2):
            vy, vz = st[w, 1, i], st[w, 2, i]
            eyz = (zn(vy) - vy) + (yn(vz) - vz)
            st[w, 8, i] = st[w, 8, i] - par[1, i] * eyz
            exx, eyy, ezz, tr = terms[i]
            if w == 1:
                for n, strain in enumerate((exx, eyy, ezz, eyz)):
                    kept[k, n, i] = strain
            else:
                a = [kept[k, n, i] for n in range(4)]
                grad[0, i] += tr * (a[0] + a[1] + a[2])
                grad[1, i] += 2.0 * (exx * a[0] + eyy * a[1] + ezz * a[2]) + eyz * a[3]
        if w == 1:
            pl.when(k == steps - 1)(lambda: go_home(2))

    def sheared(k, w):
        pl.when(has_prev)(lambda: v_ahead(k, w).wait_recv())
        pl.when(has_next)(lambda: v_back(k, w).wait_recv())
        strains = []
        for i in range(3):
            vx = edge[w, 0] if i == 0 else st[w, 0, i - 1]
            vy0 = rx_v[k, 0, w, 0] if i == 0 else st[w, 1, i - 1]
            vz0 = rx_v[k, 0, w, 1] if i == 0 else st[w, 2, i - 1]
            vy1 = rx_v[k, 1, w, 0] if i == 2 else st[w, 1, i]
            vz1 = rx_v[k, 1, w, 1] if i == 2 else st[w, 2, i]
            exy = (yn(vx) - vx) + (vy1 - vy0)
            exz = (zn(vx) - vx) + (vz1 - vz0)
            if i == 0:
                edge[w, 1] = edge[w, 1] - edge_par[0] * exy
                edge[w, 2] = edge[w, 2] - edge_par[0] * exz
            else:
                st[w, 6, i - 1] = st[w, 6, i - 1] - par[1, i - 1] * exy
                st[w, 7, i - 1] = st[w, 7, i - 1] - par[1, i - 1] * exz
                strains.append((exy, exz))
        pl.when(k < steps - 1)(lambda: transverse(k + 1, w))
        for i in range(2):
            exy, exz = strains[i]
            if w == 1:
                kept[k, 4, i] = exy
                kept[k, 5, i] = exz
            else:
                grad[1, i] += exy * kept[k, 4, i] + exz * kept[k, 5, i]
        if w == 1:
            pl.when(k == steps - 1)(lambda: go_home(3))

    def arrive(w):
        when_all(stays, local_in[w : w + 1], "wait")
        when_all(moves, wave_swap[w], "wait_recv")
        when_all(has_prev, edge_next[w], "wait_recv")
        when_all(has_next, edge_prev[w], "wait_recv")
        transverse(0, w)

    def adjoint_only(k, carry):
        normal(k, 1)
        sheared(k, 1)
        return carry

    def both(k, carry):
        normal(k, 1)
        normal(k - LEAD, 0)
        sheared(k, 1)
        sheared(k - LEAD, 0)
        return carry

    def forward_only(k, carry):
        normal(k, 0)
        sheared(k, 0)
        return carry

    arrive(1)
    lax.fori_loop(0, LEAD, adjoint_only, 0)
    arrive(0)
    lax.fori_loop(LEAD, steps, both, 0)
    lax.fori_loop(steps - LEAD, steps, forward_only, 0)

    grad[...] = DT * grad[...]
    part = ny // n_shot

    def grad_remote(t):
        return remote(
            grad.at[:, :, pl.ds(t * part, part)],
            rx_grad.at[my_shot],
            grad_send.at[t],
            grad_recv.at[my_shot],
            (jnp.int32(t), my_slab),
        )

    for t in range(n_shot):
        own = jnp.logical_and(stays, t == shot)

        @pl.when(jnp.logical_not(own))
        def _(t=t):
            grad_remote(t).start()

        @pl.when(own)
        def _(t=t):
            rx_grad[t] = grad[:, :, t * part : (t + 1) * part]

    @pl.when(moves)
    def _():
        for n in range(len(groups)):
            home_away(n).wait_recv()
            home_land(n).start()

    for t in range(n_shot):
        own = jnp.logical_and(stays, t == shot)

        @pl.when(jnp.logical_not(own))
        def _(t=t):
            remote(
                grad.at[:, :, pl.ds(t * part, part)],
                rx_grad.at[t],
                grad_send.at[t],
                grad_recv.at[t],
                (jnp.int32(t), my_slab),
            ).wait_recv()

    total = rx_grad[0]
    for t in range(1, n_shot):
        total = total + rx_grad[t]
    lam_out[...] = total[0]
    mu_out[...] = total[1]

    for t in range(n_shot):
        own = jnp.logical_and(stays, t == shot)
        pl.when(jnp.logical_not(own))(lambda t=t: grad_remote(t).wait_send())

    def drain(k, carry):
        for w in range(2):
            pl.when(has_prev)(lambda: v_back(k, w).wait_send())
            pl.when(has_next)(lambda: v_ahead(k, w).wait_send())

            @pl.when(k < steps - 1)
            def _(w=w):
                pl.when(has_prev)(lambda: s_back(k, w).wait_send())
                pl.when(has_next)(lambda: s_ahead(k, w).wait_send())

        return carry

    lax.fori_loop(0, steps, drain, 0)

    def drain_msg(t, carry):
        pl.when(jnp.logical_not(is_self(t)))(lambda: msg_copy(t).wait_send())
        return carry

    lax.fori_loop(0, n_slab, drain_msg, 0)

    when_all(sends_next, mat_edge + edge_next[0] + edge_next[1], "wait_send")
    when_all(sends_prev, edge_prev[0] + edge_prev[1], "wait_send")
    when_all(moves, mat_swap + wave_swap[0] + wave_swap[1], "wait_send")

    @pl.when(stays)
    def _():
        for n in range(len(groups)):
            home_local(n).wait()

    @pl.when(moves)
    def _():
        for n in range(len(groups)):
            home_away(n).wait_send()
            home_land(n).wait()


def deliver(a, b, c, a_out, b_out, c_out, a_mid, b_mid, c_mid, sem):
    pairs = ((a, a_mid, a_out), (b, b_mid, b_out), (c, c_mid, c_out))
    loads = [pltpu.make_async_copy(src, mid, sem.at[0, i]) for i, (src, mid, _) in enumerate(pairs)]
    stores = [pltpu.make_async_copy(mid, dst, sem.at[1, i]) for i, (_, mid, dst) in enumerate(pairs)]
    for copy in loads:
        copy.start()
    for load, store in zip(loads, stores):
        load.wait()
        store.start()
    for copy in stores:
        copy.wait()


def shards(n_shot, n_slab, lam, mu, buo, fwd, adj, wavelet, source, traces, rslab, rcell):
    planes, ny, nz = lam.shape
    steps = wavelet.shape[1]
    nrec = traces.shape[2]
    f32 = jnp.float32
    vmem = pl.BlockSpec(memory_space=pltpu.VMEM)
    hbm = pl.BlockSpec(memory_space=pl.ANY)
    dma = pltpu.SemaphoreType.DMA
    part = ny // n_shot
    outs = pl.pallas_call(
        functools.partial(kernel, n_shot, n_slab, steps),
        out_shape=(
            jax.ShapeDtypeStruct((1, 9, planes, ny, nz), f32),
            jax.ShapeDtypeStruct((planes, part, nz), f32),
            jax.ShapeDtypeStruct((planes, part, nz), f32),
        ),
        in_specs=[hbm] * 10,
        out_specs=(hbm, vmem, vmem),
        scratch_shapes=[
            pltpu.VMEM((1, steps), f32),
            pltpu.SMEM((1,), jnp.int32),
            pltpu.VMEM((1, steps, nrec), f32),
            pltpu.VMEM((1, nrec), jnp.int32),
            pltpu.VMEM((1, nrec), jnp.int32),
            dma((5,)),
            pltpu.VMEM((2, 9, planes, ny, nz), f32),
            pltpu.VMEM((3, planes, ny, nz), f32),
            pltpu.VMEM((2, 3, ny, nz), f32),
            pltpu.VMEM((2, ny, nz), f32),
            pltpu.VMEM((steps, 2, 2, ny, nz), f32),
            pltpu.VMEM((steps, 2, 2, 2, ny, nz), f32),
            pltpu.VMEM((steps, 2, 2, ny, nz), f32),
            pltpu.VMEM((steps, 2, 2, 2, ny, nz), f32),
            pltpu.VMEM((MSG, nrec), f32),
            pltpu.VMEM((n_slab, MSG, nrec), f32),
            pltpu.VMEM((steps, planes * ny, nz), f32),
            pltpu.VMEM((planes * ny, nz), f32),
            pltpu.VMEM((steps, 8, nz), f32),
            pltpu.VMEM((2, planes, ny, nz), f32),
            pltpu.VMEM((n_shot, 2, planes, part, nz), f32),
            pltpu.VMEM((steps, 6, planes, ny, nz), f32),
            pltpu.VMEM((2, 9, planes, ny, nz), f32),
            pltpu.VMEM((3, planes, ny, nz), f32),
            pltpu.VMEM((9, planes, ny, nz), f32),
            dma((5,)),
            dma((7,)),
            dma((4,)),
            dma((7,)),
            dma((5,)),
            dma((10,)),
            dma((10,)),
            dma((steps, 2, 2)),
            dma((steps, 2, 2)),
            dma((steps, 2, 2)),
            dma((steps, 2, 2)),
            dma((n_slab,)),
            dma((n_slab,)),
            dma((n_shot,)),
            dma((n_shot,)),
            dma((4,)),
            dma((4,)),
        ],
        compiler_params=pltpu.CompilerParams(
            has_side_effects=True, collective_id=0, vmem_limit_bytes=60 * 1024 * 1024
        ),
        cost_estimate=pl.CostEstimate(flops=10**7, bytes_accessed=10**6, transcendentals=0),
    )(
        lam,
        mu,
        buo,
        fwd,
        adj,
        wavelet,
        source,
        traces,
        rslab.reshape(1, nrec),
        rcell.reshape(1, nrec),
    )
    return pl.pallas_call(
        deliver,
        out_shape=tuple(jax.ShapeDtypeStruct(o.shape, o.dtype) for o in outs),
        in_specs=[hbm] * 3,
        out_specs=(hbm,) * 3,
        scratch_shapes=[pltpu.VMEM(o.shape, o.dtype) for o in outs] + [dma((2, 3))],
        compiler_params=pltpu.CompilerParams(vmem_limit_bytes=60 * 1024 * 1024),
        cost_estimate=pl.CostEstimate(flops=0, bytes_accessed=10**6, transcendentals=0),
    )(*outs)


def solution(mesh):
    in_specs = (
        P("slab", None, None),
        P("slab", None, None),
        P("slab", None, None),
        P("shot", None, "slab", None, None),
        P("shot", None, "slab", None, None),
        P("shot", None),
        P("shot"),
        P("shot", None, "slab"),
        P("slab", None),
        P("slab"),
    )
    out_specs = (
        P("shot", None, "slab", None, None),
        P("slab", "shot", None),
        P("slab", "shot", None),
    )
    body = functools.partial(shards, mesh.shape["shot"], mesh.shape["slab"])
    return jax.shard_map(body, mesh=mesh, in_specs=in_specs, out_specs=out_specs, check_vma=False)
```

```python
import functools
import jax
import jax.numpy as jnp
from jax import lax
from jax.experimental import pallas as pl
from jax.experimental.pallas import tpu as pltpu
from jax.sharding import PartitionSpec as P

DT = 0.3
MESH = pl.DeviceIdType.MESH
MSG = 16


def at_virtual(shot, slab):
    core, half = lax.rem(shot, 2), lax.rem(slab, 2)
    return (shot - core + half, slab - half + core)


def kernel(
    n_shot,
    n_slab,
    steps,
    lam_hbm,
    mu_hbm,
    buo_hbm,
    fwd_hbm,
    adj_hbm,
    wavelet_hbm,
    source_hbm,
    traces_hbm,
    rslab_hbm,
    rcell_hbm,
    adj_out,
    lam_out,
    mu_out,
    wavelet_ref,
    source_ref,
    traces_ref,
    rslab_ref,
    rcell_ref,
    small_sem,
    st,
    par,
    edge,
    edge_par,
    rx_s,
    rx_v,
    tx_s,
    tx_v,
    msg,
    rx_msg,
    push,
    spot,
    amp,
    grad,
    rx_grad,
    own,
    own_par,
    home,
    own_sem,
    swap_recv,
    home_sem,
    in_send,
    in_recv,
    edge_send,
    edge_recv,
    s_send,
    s_recv,
    v_send,
    v_recv,
    msg_send,
    msg_recv,
    grad_send,
    grad_recv,
    out_send,
    out_recv,
):
    ny, nz = st.shape[3], st.shape[4]
    cells = 2 * ny * nz
    rows = 2 * ny
    shot, slab = lax.axis_index("shot"), lax.axis_index("slab")
    my_shot, my_slab = at_virtual(shot, slab)
    stays = lax.rem(shot, 2) == lax.rem(slab, 2)
    moves = jnp.logical_not(stays)
    partner = (my_shot, my_slab)
    prev_dev = at_virtual(my_shot, jnp.maximum(my_slab - 1, 0))
    next_dev = at_virtual(my_shot, jnp.minimum(my_slab + 1, n_slab - 1))
    has_prev, has_next = my_slab > 0, my_slab < n_slab - 1

    def remote(src, dst, ssem, rsem, dev):
        return pltpu.make_async_remote_copy(
            src_ref=src, dst_ref=dst, send_sem=ssem, recv_sem=rsem, device_id=dev, device_id_type=MESH
        )

    small = [
        pltpu.make_async_copy(a, b, small_sem.at[i])
        for i, (a, b) in enumerate(
            (
                (wavelet_hbm, wavelet_ref),
                (source_hbm, source_ref),
                (traces_hbm, traces_ref),
                (rslab_hbm, rslab_ref),
                (rcell_hbm, rcell_ref),
            )
        )
    ]
    for copy in small:
        copy.start()
    own_pairs = [
        (fwd_hbm.at[0], own.at[0]),
        (adj_hbm.at[0], own.at[1]),
        (lam_hbm, own_par.at[0]),
        (mu_hbm, own_par.at[1]),
        (buo_hbm, own_par.at[2]),
    ]
    own_in = [pltpu.make_async_copy(a, b, own_sem.at[i]) for i, (a, b) in enumerate(own_pairs)]
    for copy in own_in:
        copy.start()
    work_pairs = [
        (fwd_hbm.at[0], st.at[0]),
        (adj_hbm.at[0], st.at[1]),
        (lam_hbm, par.at[0]),
        (mu_hbm, par.at[1]),
        (buo_hbm, par.at[2]),
    ]
    local_in = [pltpu.make_async_copy(a, b, in_recv.at[i]) for i, (a, b) in enumerate(work_pairs)]

    @pl.when(stays)
    def _():
        for copy in local_in:
            copy.start()

    first_shot, first_slab = shot - lax.rem(shot, 2), slab - lax.rem(slab, 2)
    barrier = pltpu.get_barrier_semaphore()

    def greet(q, carry):
        for core in range(2):
            me = jnp.logical_and(q == slab, first_shot + core == shot)

            @pl.when(jnp.logical_not(me))
            def _(core=core):
                pl.semaphore_signal(
                    barrier, inc=1, device_id=(first_shot + core, q), device_id_type=MESH
                )

        return carry

    lax.fori_loop(0, n_slab, greet, 0)
    for other in range(0, n_shot, 2):

        @pl.when(first_shot != other)
        def _(other=other):
            for t in (other, other + 1):
                for half in range(2):
                    pl.semaphore_signal(
                        barrier,
                        inc=1,
                        device_id=(jnp.int32(t), first_slab + half),
                        device_id_type=MESH,
                    )

    msg[...] = jnp.zeros_like(msg)
    for copy in small:
        copy.wait()
    msg[0:steps] = traces_ref[0]
    msg[steps : steps + 1] = rslab_ref[...].astype(jnp.float32)
    msg[steps + 1 : steps + 2] = rcell_ref[...].astype(jnp.float32)
    msg[steps + 2 : steps + 3, 0:steps] = wavelet_ref[...]
    msg[steps + 3 : steps + 4] = jnp.full((1, msg.shape[1]), source_ref[0], jnp.int32).astype(
        jnp.float32
    )

    pl.semaphore_wait(barrier, 2 * n_slab - 1 + 2 * (n_shot - 2))

    def msg_copy(t):
        return remote(msg, rx_msg.at[slab], msg_send.at[t], msg_recv.at[slab], at_virtual(shot, t))

    def msg_local():
        return pltpu.make_async_copy(msg, rx_msg.at[slab], msg_recv.at[slab])

    def is_self(t):
        return jnp.logical_and(stays, t == slab)

    def send_msg(t, carry):
        pl.when(jnp.logical_not(is_self(t)))(lambda: msg_copy(t).start())
        return carry

    lax.fori_loop(0, n_slab, send_msg, 0)
    pl.when(stays)(lambda: msg_local().start())

    orig_prev = at_virtual(shot, jnp.maximum(slab - 1, 0))
    orig_next = at_virtual(shot, jnp.minimum(slab + 1, n_slab - 1))
    sends_next, sends_prev = slab < n_slab - 1, slab > 0
    mat_next = [(own_par.at[1, 1], edge_par.at[0]), (own_par.at[2, 1], edge_par.at[1])]
    wave_next = [
        [
            (own.at[w, 6:8, 1], edge.at[w, 1:3]),
            (own.at[w, 0, 1], edge.at[w, 0]),
            (own.at[w, 3, 1], rx_s.at[0, 0, w]),
        ]
        for w in range(2)
    ]
    wave_prev = [[(own.at[w, 3, 0], rx_s.at[0, 1, w])] for w in range(2)]
    swaps = [[(own.at[w, a : a + 3], st.at[w, a : a + 3]) for a in (6, 3, 0)] for w in range(2)]

    def batch(pairs, ssem, rsem, start, dev):
        return [
            remote(a, b, ssem.at[start + n], rsem.at[start + n], dev) for n, (a, b) in enumerate(pairs)
        ]

    mat_edge = batch(mat_next, edge_send, edge_recv, 0, orig_next)
    mat_swap = batch([(own_par, par)], in_send, swap_recv, 0, partner)
    edge_next = [batch(wave_next[w], edge_send, edge_recv, 2 + 4 * w, orig_next) for w in range(2)]
    edge_prev = [batch(wave_prev[w], edge_send, edge_recv, 5 + 4 * w, orig_prev) for w in range(2)]
    wave_swap = [batch(swaps[w], in_send, swap_recv, 1 + 3 * w, partner) for w in range(2)]

    def when_all(condition, copies, action):
        @pl.when(condition)
        def _():
            for copy in copies:
                getattr(copy, action)()

    for copy in own_in[2:]:
        copy.wait()
    when_all(sends_next, mat_edge, "start")
    when_all(moves, mat_swap, "start")
    for w in range(2):
        own_in[w].wait()
        when_all(sends_next, edge_next[w], "start")
        when_all(sends_prev, edge_prev[w], "start")
        when_all(moves, wave_swap[w], "start")

    @pl.when(jnp.logical_not(has_prev))
    def _():
        edge[...] = jnp.zeros_like(edge)
        edge_par[...] = jnp.zeros_like(edge_par)
        rx_s[:, 0] = jnp.zeros((steps, 2, ny, nz), jnp.float32)
        rx_v[:, 0] = jnp.zeros((steps, 2, 2, ny, nz), jnp.float32)

    @pl.when(jnp.logical_not(has_next))
    def _():
        rx_s[:, 1] = jnp.zeros((steps, 2, ny, nz), jnp.float32)
        rx_v[:, 1] = jnp.zeros((steps, 2, 2, ny, nz), jnp.float32)

    grad[...] = jnp.zeros_like(grad)
    push[...] = jnp.zeros_like(push)

    nrec = msg.shape[1]
    row_of = lax.broadcasted_iota(jnp.int32, (rows, nrec), 0)
    col_of = lax.broadcasted_iota(jnp.int32, (nz, nrec), 0)

    def scatter(pair, carry):
        left, right = [], []
        for q in (2 * pair, 2 * pair + 1):
            pltpu.make_async_copy(msg, rx_msg.at[q], msg_recv.at[q]).wait()
            block = rx_msg[q]
            named = block[steps : steps + 1].astype(jnp.int32)
            cell = block[steps + 1 : steps + 2].astype(jnp.int32)
            row = jnp.where(named == my_slab, cell // nz, -1)
            hit = row_of == row
            column = (col_of == lax.rem(cell, nz)).astype(jnp.float32).astype(jnp.bfloat16)
            trace = block[0:steps]
            high = trace.astype(jnp.bfloat16).astype(jnp.float32)
            low = trace - high
            left.append(
                jnp.concatenate(
                    [
                        jnp.where(hit, term[k : k + 1], 0.0).astype(jnp.bfloat16)
                        for term in (high, low)
                        for k in range(steps)
                    ],
                    axis=0,
                )
            )
            right.append(column)
        out = lax.dot_general(
            jnp.concatenate(left, axis=1),
            jnp.concatenate(right, axis=1),
            (((1,), (1,)), ((), ())),
            preferred_element_type=jnp.float32,
        )
        for k in range(steps):
            push[k] += out[k * rows : (k + 1) * rows] + out[(steps + k) * rows : (steps + k + 1) * rows]
        return carry

    blocks = n_slab // 2
    lax.fori_loop(0, blocks - 2, scatter, 0)

    when_all(stays, local_in[2:], "wait")
    when_all(moves, mat_swap, "wait_recv")
    when_all(has_prev, mat_edge, "wait_recv")

    y_at = lax.broadcasted_iota(jnp.int32, (ny, nz), 0)
    z_at = lax.broadcasted_iota(jnp.int32, (ny, nz), 1)

    def yn(a):
        return jnp.where(y_at < ny - 1, pltpu.roll(a, ny - 1, 0), 0.0)

    def yp(a):
        return jnp.where(y_at > 0, pltpu.roll(a, 1, 0), 0.0)

    def zn(a):
        return jnp.where(z_at < nz - 1, pltpu.roll(a, nz - 1, 1), 0.0)

    def zp(a):
        return jnp.where(z_at > 0, pltpu.roll(a, 1, 1), 0.0)

    par[0] = DT * par[0]
    par[1] = DT * par[1]
    par[2] = DT * par[2]
    edge_par[...] = DT * edge_par[...]

    def v_back(k, w):
        return remote(
            tx_v.at[k, 0, w], rx_v.at[k, 1, w], v_send.at[k, 0, w], v_recv.at[k, 1, w], prev_dev
        )

    def v_ahead(k, w):
        return remote(
            tx_v.at[k, 1, w], rx_v.at[k, 0, w], v_send.at[k, 1, w], v_recv.at[k, 0, w], next_dev
        )

    def s_back(k, w):
        return remote(
            tx_s.at[k, 0, w], rx_s.at[k, 1, w], s_send.at[k, 0, w], s_recv.at[k, 1, w], prev_dev
        )

    def s_ahead(k, w):
        return remote(
            tx_s.at[k, 1, w], rx_s.at[k, 0, w], s_send.at[k, 1, w], s_recv.at[k, 0, w], next_dev
        )

    groups = ((0, 3), (3, 6), (8, 9), (6, 8))

    def home_local(n):
        a, b = groups[n]
        return pltpu.make_async_copy(st.at[1, a:b], adj_out.at[0, a:b], home_sem.at[n])

    def home_land(n):
        a, b = groups[n]
        return pltpu.make_async_copy(home.at[a:b], adj_out.at[0, a:b], home_sem.at[n])

    def home_away(n):
        a, b = groups[n]
        return remote(st.at[1, a:b], home.at[a:b], out_send.at[n], out_recv.at[n], partner)

    def go_home(n):
        pl.when(stays)(lambda: home_local(n).start())
        pl.when(moves)(lambda: home_away(n).start())

    def transverse(k, w):
        for i in range(2):
            sxy0 = edge[w, 1] if i == 0 else st[w, 6, 0]
            sxz0 = edge[w, 2] if i == 0 else st[w, 7, 0]
            syy, szz, syz = st[w, 4, i], st[w, 5, i], st[w, 8, i]
            vy = st[w, 1, i] - par[2, i] * (
                (st[w, 6, i] - sxy0) + (yn(syy) - syy) + (syz - zp(syz))
            )
            vz = st[w, 2, i] - par[2, i] * (
                (st[w, 7, i] - sxz0) + (syz - yp(syz)) + (zn(szz) - szz)
            )
            st[w, 1, i] = vy
            st[w, 2, i] = vz
            tx_v[k, i, w, 0] = vy
            tx_v[k, i, w, 1] = vz
        pl.when(has_prev)(lambda: v_back(k, w).start())
        pl.when(has_next)(lambda: v_ahead(k, w).start())

    def step(k, carry):
        normal = []
        for w in range(2):
            @pl.when(k > 0)
            def _(w=w):
                pl.when(has_prev)(lambda: s_ahead(k, w).wait_recv())
                pl.when(has_next)(lambda: s_back(k, w).wait_recv())

            sxx = [rx_s[k, 0, w], st[w, 3, 0], st[w, 3, 1], rx_s[k, 1, w]]
            for i in range(3):
                sxy = edge[w, 1] if i == 0 else st[w, 6, i - 1]
                sxz = edge[w, 2] if i == 0 else st[w, 7, i - 1]
                factor = edge_par[1] if i == 0 else par[2, i - 1]
                change = factor * ((sxx[i + 1] - sxx[i]) + (sxy - yp(sxy)) + (sxz - zp(sxz)))
                if i == 0:
                    edge[w, 0] = edge[w, 0] - change
                else:
                    st[w, 0, i - 1] = st[w, 0, i - 1] - change

            terms = []
            for i in range(2):
                at = pl.ds(i * ny, ny)
                gain = amp[k, 0:1] * spot[at] if w == 0 else DT * push[k, at]
                vx0 = edge[w, 0] if i == 0 else st[w, 0, 0]
                vy, vz = st[w, 1, i], st[w, 2, i]
                exx = st[w, 0, i] - vx0
                eyy = vy - yp(vy)
                ezz = vz - zp(vz)
                tr = exx + eyy + ezz
                common = par[0, i] * tr + gain
                twice = 2.0 * par[1, i]
                new = st[w, 3, i] - (common + twice * exx)
                st[w, 3, i] = new
                tx_s[k, i, w] = new
                st[w, 4, i] = st[w, 4, i] - (common + twice * eyy)
                st[w, 5, i] = st[w, 5, i] - (common + twice * ezz)
                terms.append((exx, eyy, ezz, tr))
            normal.append(terms)

            @pl.when(k < steps - 1)
            def _(w=w):
                back = remote(
                    tx_s.at[k, 0, w],
                    rx_s.at[k + 1, 1, w],
                    s_send.at[k, 0, w],
                    s_recv.at[k + 1, 1, w],
                    prev_dev,
                )
                ahead = remote(
                    tx_s.at[k, 1, w],
                    rx_s.at[k + 1, 0, w],
                    s_send.at[k, 1, w],
                    s_recv.at[k + 1, 0, w],
                    next_dev,
                )
                pl.when(has_prev)(lambda: back.start())
                pl.when(has_next)(lambda: ahead.start())

        @pl.when(k == steps - 1)
        def _():
            go_home(0)
            go_home(1)

        for i in range(2):
            f, a = normal[0][i], normal[1][i]
            grad[0, i] += f[3] * a[3]
            eyz = []
            for w in range(2):
                vy, vz = st[w, 1, i], st[w, 2, i]
                strain = (zn(vy) - vy) + (yn(vz) - vz)
                st[w, 8, i] = st[w, 8, i] - par[1, i] * strain
                eyz.append(strain)
            grad[1, i] += 2.0 * (f[0] * a[0] + f[1] * a[1] + f[2] * a[2]) + eyz[0] * eyz[1]

        pl.when(k == steps - 1)(lambda: go_home(2))

        shear = []
        for w in range(2):
            pl.when(has_prev)(lambda: v_ahead(k, w).wait_recv())
            pl.when(has_next)(lambda: v_back(k, w).wait_recv())
            strains = []
            for i in range(3):
                vx = edge[w, 0] if i == 0 else st[w, 0, i - 1]
                vy0 = rx_v[k, 0, w, 0] if i == 0 else st[w, 1, i - 1]
                vz0 = rx_v[k, 0, w, 1] if i == 0 else st[w, 2, i - 1]
                vy1 = rx_v[k, 1, w, 0] if i == 2 else st[w, 1, i]
                vz1 = rx_v[k, 1, w, 1] if i == 2 else st[w, 2, i]
                exy = (yn(vx) - vx) + (vy1 - vy0)
                exz = (zn(vx) - vx) + (vz1 - vz0)
                if i == 0:
                    edge[w, 1] = edge[w, 1] - edge_par[0] * exy
                    edge[w, 2] = edge[w, 2] - edge_par[0] * exz
                else:
                    st[w, 6, i - 1] = st[w, 6, i - 1] - par[1, i - 1] * exy
                    st[w, 7, i - 1] = st[w, 7, i - 1] - par[1, i - 1] * exz
                    strains.append((exy, exz))
            shear.append(strains)
            pl.when(k < steps - 1)(lambda w=w: transverse(k + 1, w))

        for i in range(2):
            f, a = shear[0][i], shear[1][i]
            grad[1, i] += f[0] * a[0] + f[1] * a[1]
        return carry

    for w in range(2):
        when_all(stays, local_in[w : w + 1], "wait")
        when_all(moves, wave_swap[w], "wait_recv")
        when_all(has_prev, edge_next[w], "wait_recv")
        when_all(has_next, edge_prev[w], "wait_recv")
        transverse(0, w)
        lax.fori_loop(blocks - 2 + w, blocks - 1 + w, scatter, 0)
    head = rx_msg[my_slab]
    source = head[steps + 3 : steps + 4].astype(jnp.int32) - my_slab * cells
    flat = lax.broadcasted_iota(jnp.int32, (rows, nz), 0) * nz
    flat = flat + lax.broadcasted_iota(jnp.int32, (rows, nz), 1)
    spot[...] = (flat == source).astype(jnp.float32)
    for k in range(steps):
        amp[k] = jnp.broadcast_to(DT * head[steps + 2 : steps + 3, k : k + 1], (8, nz))

    lax.fori_loop(0, steps, step, 0)

    go_home(3)
    grad[...] = DT * grad[...]
    part = ny // n_shot

    def grad_remote(t):
        return remote(
            grad.at[:, :, pl.ds(t * part, part)],
            rx_grad.at[my_shot],
            grad_send.at[t],
            grad_recv.at[my_shot],
            (jnp.int32(t), my_slab),
        )

    for t in range(n_shot):
        own = jnp.logical_and(stays, t == shot)

        @pl.when(jnp.logical_not(own))
        def _(t=t):
            grad_remote(t).start()

        @pl.when(own)
        def _(t=t):
            rx_grad[t] = grad[:, :, t * part : (t + 1) * part]

    @pl.when(moves)
    def _():
        for n in range(len(groups)):
            home_away(n).wait_recv()
            home_land(n).start()

    for t in range(n_shot):
        own = jnp.logical_and(stays, t == shot)

        @pl.when(jnp.logical_not(own))
        def _(t=t):
            remote(
                grad.at[:, :, pl.ds(t * part, part)],
                rx_grad.at[t],
                grad_send.at[t],
                grad_recv.at[t],
                (jnp.int32(t), my_slab),
            ).wait_recv()

    total = rx_grad[0]
    for t in range(1, n_shot):
        total = total + rx_grad[t]
    lam_out[...] = total[0]
    mu_out[...] = total[1]

    for t in range(n_shot):
        own = jnp.logical_and(stays, t == shot)
        pl.when(jnp.logical_not(own))(lambda t=t: grad_remote(t).wait_send())

    def drain(k, carry):
        for w in range(2):
            pl.when(has_prev)(lambda: v_back(k, w).wait_send())
            pl.when(has_next)(lambda: v_ahead(k, w).wait_send())

            @pl.when(k < steps - 1)
            def _(w=w):
                pl.when(has_prev)(lambda: s_back(k, w).wait_send())
                pl.when(has_next)(lambda: s_ahead(k, w).wait_send())

        return carry

    lax.fori_loop(0, steps, drain, 0)

    def drain_msg(t, carry):
        pl.when(jnp.logical_not(is_self(t)))(lambda: msg_copy(t).wait_send())
        return carry

    lax.fori_loop(0, n_slab, drain_msg, 0)

    when_all(sends_next, mat_edge + edge_next[0] + edge_next[1], "wait_send")
    when_all(sends_prev, edge_prev[0] + edge_prev[1], "wait_send")
    when_all(moves, mat_swap + wave_swap[0] + wave_swap[1], "wait_send")

    @pl.when(stays)
    def _():
        for n in range(len(groups)):
            home_local(n).wait()

    @pl.when(moves)
    def _():
        for n in range(len(groups)):
            home_away(n).wait_send()
            home_land(n).wait()


def deliver(a, b, c, a_out, b_out, c_out, a_mid, b_mid, c_mid, sem):
    pairs = ((a, a_mid, a_out), (b, b_mid, b_out), (c, c_mid, c_out))
    loads = [pltpu.make_async_copy(src, mid, sem.at[0, i]) for i, (src, mid, _) in enumerate(pairs)]
    stores = [pltpu.make_async_copy(mid, dst, sem.at[1, i]) for i, (_, mid, dst) in enumerate(pairs)]
    for copy in loads:
        copy.start()
    for load, store in zip(loads, stores):
        load.wait()
        store.start()
    for copy in stores:
        copy.wait()


def shards(n_shot, n_slab, lam, mu, buo, fwd, adj, wavelet, source, traces, rslab, rcell):
    planes, ny, nz = lam.shape
    steps = wavelet.shape[1]
    nrec = traces.shape[2]
    f32 = jnp.float32
    vmem = pl.BlockSpec(memory_space=pltpu.VMEM)
    hbm = pl.BlockSpec(memory_space=pl.ANY)
    dma = pltpu.SemaphoreType.DMA
    part = ny // n_shot
    outs = pl.pallas_call(
        functools.partial(kernel, n_shot, n_slab, steps),
        out_shape=(
            jax.ShapeDtypeStruct((1, 9, planes, ny, nz), f32),
            jax.ShapeDtypeStruct((planes, part, nz), f32),
            jax.ShapeDtypeStruct((planes, part, nz), f32),
        ),
        in_specs=[hbm] * 10,
        out_specs=(hbm, vmem, vmem),
        scratch_shapes=[
            pltpu.VMEM((1, steps), f32),
            pltpu.SMEM((1,), jnp.int32),
            pltpu.VMEM((1, steps, nrec), f32),
            pltpu.VMEM((1, nrec), jnp.int32),
            pltpu.VMEM((1, nrec), jnp.int32),
            dma((5,)),
            pltpu.VMEM((2, 9, planes, ny, nz), f32),
            pltpu.VMEM((3, planes, ny, nz), f32),
            pltpu.VMEM((2, 3, ny, nz), f32),
            pltpu.VMEM((2, ny, nz), f32),
            pltpu.VMEM((steps, 2, 2, ny, nz), f32),
            pltpu.VMEM((steps, 2, 2, 2, ny, nz), f32),
            pltpu.VMEM((steps, 2, 2, ny, nz), f32),
            pltpu.VMEM((steps, 2, 2, 2, ny, nz), f32),
            pltpu.VMEM((MSG, nrec), f32),
            pltpu.VMEM((n_slab, MSG, nrec), f32),
            pltpu.VMEM((steps, planes * ny, nz), f32),
            pltpu.VMEM((planes * ny, nz), f32),
            pltpu.VMEM((steps, 8, nz), f32),
            pltpu.VMEM((2, planes, ny, nz), f32),
            pltpu.VMEM((n_shot, 2, planes, part, nz), f32),
            pltpu.VMEM((2, 9, planes, ny, nz), f32),
            pltpu.VMEM((3, planes, ny, nz), f32),
            pltpu.VMEM((9, planes, ny, nz), f32),
            dma((5,)),
            dma((7,)),
            dma((4,)),
            dma((7,)),
            dma((5,)),
            dma((10,)),
            dma((10,)),
            dma((steps, 2, 2)),
            dma((steps, 2, 2)),
            dma((steps, 2, 2)),
            dma((steps, 2, 2)),
            dma((n_slab,)),
            dma((n_slab,)),
            dma((n_shot,)),
            dma((n_shot,)),
            dma((4,)),
            dma((4,)),
        ],
        compiler_params=pltpu.CompilerParams(
            has_side_effects=True, collective_id=0, vmem_limit_bytes=60 * 1024 * 1024
        ),
        cost_estimate=pl.CostEstimate(flops=10**7, bytes_accessed=10**6, transcendentals=0),
    )(
        lam,
        mu,
        buo,
        fwd,
        adj,
        wavelet,
        source,
        traces,
        rslab.reshape(1, nrec),
        rcell.reshape(1, nrec),
    )
    return pl.pallas_call(
        deliver,
        out_shape=tuple(jax.ShapeDtypeStruct(o.shape, o.dtype) for o in outs),
        in_specs=[hbm] * 3,
        out_specs=(hbm,) * 3,
        scratch_shapes=[pltpu.VMEM(o.shape, o.dtype) for o in outs] + [dma((2, 3))],
        compiler_params=pltpu.CompilerParams(vmem_limit_bytes=60 * 1024 * 1024),
        cost_estimate=pl.CostEstimate(flops=0, bytes_accessed=10**6, transcendentals=0),
    )(*outs)


def solution(mesh):
    in_specs = (
        P("slab", None, None),
        P("slab", None, None),
        P("slab", None, None),
        P("shot", None, "slab", None, None),
        P("shot", None, "slab", None, None),
        P("shot", None),
        P("shot"),
        P("shot", None, "slab"),
        P("slab", None),
        P("slab"),
    )
    out_specs = (
        P("shot", None, "slab", None, None),
        P("slab", "shot", None),
        P("slab", "shot", None),
    )
    body = functools.partial(shards, mesh.shape["shot"], mesh.shape["slab"])
    return jax.shard_map(body, mesh=mesh, in_specs=in_specs, out_specs=out_specs, check_vma=False)
```
